128 devices in a mesh: ctx: 32 (over x, y, z_hi), mem: 4 (over z_lo, core).
Axes of the slice: x: 4, y: 4, z: 4 (z_hi: 2, z_lo: 2; z = z_hi * 2 + z_lo), core: 2. Of those that a mesh axis runs over, the one named last changes fastest.
Arguments:
- queries: bfloat16 [8192, 4096], P('ctx', 'mem')
- keys: bfloat16 [8192, 1024], P('ctx', 'mem')
- values: bfloat16 [8192, 1024], P('ctx', 'mem'), may hold values from -6 to 6
- mem_keys: bfloat16 [1024, 64, 1024], P('ctx', None, 'mem')
- mem_values: bfloat16 [1024, 64, 1024], P('ctx', None, 'mem'), may hold values from -6 to 6
- retrieval: int32 [64, 4, 32], P('ctx', 'mem'), may hold values from 0 to 1023, as said below
- gate_weight: bfloat16 [2, 4096, 32], P(None, 'mem'), may hold values from -0.375 to 0.375
- gate_bias: float32 [32], P('mem'), may hold values from -2 to 2
Outputs:
- mixed: bfloat16 [8192, 4096], P('ctx', 'mem')
The draws below stay inside these ranges and needn't reach their ends.
Inputs may be any that keep to these rules, and one draw needn't show every extreme that they name: Each list retrieval[b, g] names 32 distinct blocks. At most 2 of them lie in one shard of 32 consecutive blocks; one shard, the same for all lists, holds exactly 2 blocks of every list.
All inputs are finite; a program needn't handle non-finite values.
Results may differ from the reference program's by a relative error of at most 0.013.
Values may be sent and summed in bfloat16 or wider, within the bound.
A program may use at most 192 MiB of HBM per device.

```python
import jax
import jax.numpy as jnp
from jax import lax

HEADS = 32
KVH = 8
DH = 128
QBLK = 128
MBLK = 64
TOPB = 32
MB_DEV = 32
TOKENS = 8192
QBLOCKS = 64
MEMB = 1024
HPG = 8
CAP = 2
N_CTX = 32
N_MEM = 4


def local_keys(key):
    width = KVH * DH
    base = jax.random.normal(jax.random.fold_in(key, 5), (TOKENS, width), jnp.float32)
    return base


def memory_rows(key, blocks):
    width = KVH * DH
    key_rows = jax.random.fold_in(key, 7)

    def one_block(block):
        rows = jax.random.normal(jax.random.fold_in(key_rows, block), (MBLK, width), jnp.float32)
        return rows.at[2].set(rows[2])
    return jax.vmap(one_block)(blocks)


def retrieval_lists(key):
    hot = jax.random.randint(jax.random.fold_in(key, 12), (), 0, N_CTX)
    off_scores = jax.random.randint(jax.random.fold_in(key, 13), (QBLOCKS, N_MEM, N_CTX, MB_DEV), 0, 4096)
    off_scores = off_scores * MB_DEV + jnp.arange(MB_DEV, dtype=jnp.int32)
    _, offsets = lax.top_k(off_scores, CAP)
    priority = jax.random.randint(jax.random.fold_in(key, 14), (QBLOCKS, N_MEM, N_CTX, CAP), 0, 65536)
    priority = priority * (N_CTX * CAP) + jnp.arange(N_CTX * CAP, dtype=jnp.int32).reshape(N_CTX, CAP)
    owners = jnp.arange(N_CTX, dtype=jnp.int32)[:, None]
    priority = priority + jnp.where(owners == hot, 1 << 26, 0).astype(jnp.int32)
    _, picked = lax.top_k(priority.reshape(QBLOCKS, N_MEM, N_CTX * CAP), TOPB)
    owner = picked // CAP
    offset = jnp.take_along_axis(offsets.reshape(QBLOCKS, N_MEM, N_CTX * CAP), picked, axis=2)
    return (owner * MB_DEV + offset).astype(jnp.int32)


def draw_keys(key, part):
    result = local_keys(key)
    return result.astype(jnp.bfloat16)


def draw_mem_keys(key, part):
    result = memory_rows(key, jnp.arange(MEMB, dtype=jnp.int32))
    return result.astype(jnp.bfloat16)


def draw_retrieval(key, part):
    return retrieval_lists(key)


def draw_queries(key, part):
    own = jax.random.fold_in(key, 41)
    width = HEADS * DH
    result = 2.0 * jax.random.normal(own, (TOKENS, width), jnp.float32)
    return result.astype(jnp.bfloat16)


def steps_of(key, dims, cuts, smallest, top_value):
    loudness = 1.0
    for dim, blocks in cuts:
        heights = jax.random.uniform(jax.random.fold_in(jax.random.fold_in(key, 6), dim), (blocks,), jnp.float32, smallest / len(cuts), top_value / len(cuts))
        loudness = loudness * jnp.repeat(jnp.exp(heights), dims[dim] // blocks).reshape((-1,) + (1,) * (len(dims) - 1 - dim))
    return loudness


def scatter_about(stream_key, shape, scale, reach, cuts=(), kind=jnp.bfloat16):
    loudness = steps_of(stream_key, shape, cuts, -0.22, 0.18) if cuts else 1.0
    array = jax.random.normal(stream_key, shape, jnp.float32) * scale * loudness
    return jnp.minimum(jnp.maximum(array, -reach), reach).astype(kind)


def setup_inputs(seed: int = 0) -> dict:
    key_of = jax.random.split(jax.random.key(seed), 9)
    return {
        "queries": draw_queries(jax.random.fold_in(key_of[8], 71), 0),
        "keys": draw_keys(jax.random.fold_in(key_of[8], 71), 0),
        "values": scatter_about(key_of[2], (TOKENS, KVH * DH), 1.0, 6.0, ((0, 32), (1, 4))),
        "mem_keys": draw_mem_keys(jax.random.fold_in(key_of[8], 71), 0),
        "mem_values": scatter_about(key_of[4], (MEMB, MBLK, KVH * DH), 1.0, 6.0, ((0, 32), (2, 4))),
        "retrieval": draw_retrieval(jax.random.fold_in(key_of[8], 71), 0),
        "gate_weight": scatter_about(key_of[6], (2, HEADS * DH, HEADS), (HEADS * DH // 16) ** -0.5, 0.375, ((1, 4),)),
        "gate_bias": jnp.clip(jax.random.uniform(key_of[7], (HEADS,), jnp.float32, -2.0, 2.0) * steps_of(key_of[7], (HEADS,), ((0, 4),), -0.4, 0.0), -2.0, 2.0),
    }


def reference(queries, keys, values, mem_keys, mem_values, retrieval, gate_weight, gate_bias):
    scale = DH ** -0.5
    width = HEADS * DH
    share_count = HEADS // KVH
    kv_group = KVH // N_MEM
    q_heads = queries.astype(jnp.float32).reshape(TOKENS, KVH, share_count, DH).transpose(1, 2, 0, 3)
    k_heads = keys.astype(jnp.float32).reshape(TOKENS, KVH, DH).transpose(1, 0, 2)
    v_heads = values.astype(jnp.float32).reshape(TOKENS, KVH, DH).transpose(1, 0, 2)
    position = jnp.arange(TOKENS, dtype=jnp.int32)
    span = TOKENS // 8

    def local_head(operands):
        q_one, k_one, v_one = operands
        outputs = []
        for piece in range(8):
            first = piece * span
            limit = first + span
            q_part = q_one[:, first:limit]
            scores = jnp.einsum("gtd,pd->gtp", q_part, k_one[:limit]) * scale
            visible = (position[:limit] // QBLK)[None, :] <= (position[first:limit] // QBLK)[:, None]
            scores = jnp.where(visible[None], scores, -jnp.inf)
            top = jnp.max(scores, axis=2, keepdims=True)
            weights = jnp.exp(scores - top)
            total = jnp.sum(weights, axis=2, keepdims=True)
            rounded = lax.optimization_barrier(weights.astype(jnp.bfloat16)).astype(jnp.float32)
            outputs.append(jnp.einsum("gtp,pd->gtd", rounded, v_one[:limit]) / total)
        return jnp.concatenate(outputs, axis=1)

    local = lax.map(local_head, (q_heads, k_heads, v_heads))
    local_tok = local.transpose(2, 0, 1, 3).reshape(TOKENS, width)

    q_blocks = queries.astype(jnp.float32).reshape(QBLOCKS, QBLK, HEADS, DH)

    def memory_block(operands):
        q_block, lists = operands
        pieces = []
        for group in range(N_MEM):
            cols = slice(group * kv_group * DH, (group + 1) * kv_group * DH)
            block_keys = mem_keys[lists[group]][:, :, cols].astype(jnp.float32).reshape(TOPB * MBLK, kv_group, DH)
            block_vals = mem_values[lists[group]][:, :, cols].astype(jnp.float32).reshape(TOPB * MBLK, kv_group, DH)
            q_group = q_block[:, group * HPG:(group + 1) * HPG].reshape(QBLK, kv_group, share_count, DH)
            scores = jnp.einsum("qkgd,skd->kgqs", q_group, block_keys) * scale
            top = jnp.max(scores, axis=3, keepdims=True)
            weights = jnp.exp(scores - top)
            total = jnp.sum(weights, axis=3, keepdims=True)
            rounded = lax.optimization_barrier(weights.astype(jnp.bfloat16)).astype(jnp.float32)
            result = jnp.einsum("kgqs,skd->kgqd", rounded, block_vals) / total
            pieces.append(result.transpose(2, 0, 1, 3).reshape(QBLK, HPG, DH))
        return jnp.concatenate(pieces, axis=1)

    memory = lax.map(memory_block, (q_blocks, retrieval))
    memory_tok = memory.reshape(TOKENS, width)

    logits = jnp.dot(local_tok.astype(jnp.bfloat16), gate_weight[0], preferred_element_type=jnp.float32)
    logits = logits + jnp.dot(memory_tok.astype(jnp.bfloat16), gate_weight[1], preferred_element_type=jnp.float32)
    logits = logits + gate_bias[None, :]
    share = jax.nn.sigmoid(logits)[:, :, None]
    mixed = share * memory_tok.reshape(TOKENS, HEADS, DH) + (1.0 - share) * local_tok.reshape(TOKENS, HEADS, DH)
    return mixed.reshape(TOKENS, width).astype(jnp.bfloat16)
```

```python
import functools
import math

import jax
import jax.numpy as jnp
from jax import lax
from jax.experimental import pallas as pl
from jax.experimental.pallas import tpu as pltpu
from jax.sharding import PartitionSpec as P

MESH = pl.DeviceIdType.MESH
SIDE = 4
DH = 128
SHARE = 4
QBLK = 128
ROWS = 256
SHARD_BLOCKS = 32
MBLK = 64
GROUPS = 4
HEADS_DEV = 8
NEG = -1e30
FACTOR = DH**-0.5 * math.log2(math.e)


def dot_nt(a, b):
    return lax.dot_general(a, b, (((1,), (1,)), ((), ())), preferred_element_type=jnp.float32)


def with_ones(v):
    return jnp.concatenate([v, jnp.ones_like(v)], axis=1)


def rows_of(column_wide):
    eye = lax.broadcasted_iota(jnp.int32, (QBLK, QBLK), 0) == lax.broadcasted_iota(
        jnp.int32, (QBLK, QBLK), 1
    )
    pieces = []
    for g in range(SHARE):
        part = column_wide[g * QBLK : (g + 1) * QBLK]
        pieces.append(jnp.sum(jnp.where(eye, part, 0.0), axis=0, keepdims=True))
    pieces.append(jnp.zeros((8 - SHARE, QBLK), jnp.float32))
    return jnp.concatenate(pieces, axis=0)


def kernel(
    q_hbm, k_hbm, v_hbm, mk_hbm, mv_hbm, tab_hbm, gw_ref, gb_ref,
    out_ref,
    q_buf, kv_buf, mem_buf, tab_buf, tab_sm,
    loc_part, loc_lse, loc_in, loc_lse_in,
    mem_part, mem_lse, mem_in, mem_lse_in,
    z_part, z_lse, z_in, z_lse_in,
    loc_fin, mem_fin, acc_ref, max_ref, lg_out, lg_in,
    l_sem, kvz_s, kvz_r, kva_s, kva_r, qb_s, qb_r, qz_s, qz_r, tab_s, tab_r, ma_s, ma_r,
    lo_s, lo_r, ls_s, ls_r, me_s, me_r, ms_s, ms_r, z_s, z_r, zs_s, zs_r, lg_s, lg_r,
):
    c = lax.axis_index("ctx")
    g_own = lax.axis_index("mem")
    x, y, z = c // 8, (c // 2) % 4, c % 2
    zo = 1 - z

    def wrap(i):
        return lax.rem(i + SIDE, SIDE)

    def device(px, py, pz):
        return (px * 8 + py * 2 + pz, g_own)

    def key_peer(h, d):
        return device(wrap(x + d), y, z) if h == 0 else device(x, wrap(y + d), z)

    def query_peer(h, d):
        return key_peer(1 - h, d)

    z_peer = device(x, y, zo)
    a_own = (x, y)
    b_own = (y, x)

    def remote(src, dst, ssem, rsem, peer):
        return pltpu.make_async_remote_copy(
            src_ref=src, dst_ref=dst, send_sem=ssem, recv_sem=rsem,
            device_id=peer, device_id_type=MESH,
        )

    kv_local, q_local, mem_local, tab_local = [], [], [], []
    count = 0

    def local(src, dst, group):
        nonlocal count
        cp = pltpu.make_async_copy(src, dst, l_sem.at[count])
        cp.start()
        group.append(cp)
        count += 1

    for h in range(2):
        cols = pl.ds(h * DH, DH)
        local(k_hbm.at[:, cols], kv_buf.at[h, a_own[h], 0, z], kv_local)
        local(v_hbm.at[:, cols], kv_buf.at[h, a_own[h], 1, z], kv_local)
    for h in range(2):
        for g in range(SHARE):
            local(
                q_hbm.at[:, pl.ds((h * SHARE + g) * DH, DH)],
                q_buf.at[h, b_own[h], z, g],
                q_local,
            )
        local(tab_hbm, tab_buf.at[h, b_own[h], z], tab_local)
    for h in range(2):
        cols = pl.ds(h * DH, DH)
        local(mk_hbm.at[:, :, cols], mem_buf.at[h, a_own[h], 0], mem_local)
        local(mv_hbm.at[:, :, cols], mem_buf.at[h, a_own[h], 1], mem_local)

    barrier = pltpu.get_barrier_semaphore()
    greeted = [z_peer]
    for d in range(1, SIDE):
        greeted += [device(wrap(x + d), y, z), device(x, wrap(y + d), z)]
        greeted += [device(wrap(x + d), y, zo), device(x, wrap(y + d), zo)]
        greeted += [(c, lax.rem(g_own + d, GROUPS))]
    for peer in greeted:
        pl.semaphore_signal(barrier, inc=1, device_id=peer, device_id_type=MESH)
    pl.semaphore_wait(barrier, len(greeted))

    started = []

    def go(cp):
        cp.start()
        started.append(cp)
        return cp

    def kv_z(h):
        ref = kv_buf.at[h, a_own[h], :, z]
        return remote(ref, ref, kvz_s.at[h], kvz_r.at[h], z_peer)

    def kv_z_in(h):
        ref = kv_buf.at[h, a_own[h], :, zo]
        return remote(ref, ref, kvz_s.at[h], kvz_r.at[h], z_peer)

    def kv_a(h, part, d):
        ref = kv_buf.at[h, a_own[h], :, (z, zo)[part]]
        return remote(ref, ref, kva_s.at[h, part, d], kva_r.at[h, part, d], key_peer(h, d))

    def kv_a_in(h, part, d):
        ref = kv_buf.at[h, wrap(a_own[h] - d), :, (z, zo)[part]]
        return remote(ref, ref, kva_s.at[h, part, d], kva_r.at[h, part, d], key_peer(h, d))

    def q_b(h, d):
        ref = q_buf.at[h, b_own[h], z]
        return remote(ref, ref, qb_s.at[h, d], qb_r.at[h, d], query_peer(h, d))

    def q_b_in(h, d):
        ref = q_buf.at[h, wrap(b_own[h] - d), z]
        return remote(ref, ref, qb_s.at[h, d], qb_r.at[h, d], query_peer(h, d))

    def q_z(h, d):
        ref = q_buf.at[h, wrap(b_own[h] + d), z]
        return remote(ref, ref, qz_s.at[h, d], qz_r.at[h, d], z_peer)

    def q_z_in(h, d):
        ref = q_buf.at[h, wrap(b_own[h] + d), zo]
        return remote(ref, ref, qz_s.at[h, d], qz_r.at[h, d], z_peer)

    def tab_peer(h, d, dz):
        pz = zo if dz else z
        return device(x, wrap(y + d), pz) if h == 0 else device(wrap(x + d), y, pz)

    def tab(h, d, dz):
        ref = tab_buf.at[h, b_own[h], z]
        sem = d * 2 + dz
        return remote(ref, ref, tab_s.at[h, sem], tab_r.at[h, sem], tab_peer(h, d, dz))

    def tab_in(h, d, dz):
        ref = tab_buf.at[h, wrap(b_own[h] - d), zo if dz else z]
        sem = d * 2 + dz
        return remote(ref, ref, tab_s.at[h, sem], tab_r.at[h, sem], tab_peer(h, d, dz))

    def mem_copy(h, which, ref, d):
        return remote(ref, ref, ma_s.at[h, which], ma_r.at[h, which], key_peer(h, d))

    for cp in kv_local:
        cp.wait()
    for h in range(2):
        go(kv_z(h))
    for d in (2, 1, 3):
        for h in range(2):
            go(kv_a(h, 0, d))
    for cp in q_local:
        cp.wait()
    for d in (2, 1, 3):
        for h in range(2):
            go(q_b(h, d))
    for h in range(2):
        go(q_z(h, 0))
    for cp in tab_local:
        cp.wait()
    for h in range(2):
        for d in range(SIDE):
            for dz in range(2):
                if d or dz:
                    go(tab(h, d, dz))
    for cp in mem_local:
        cp.wait()
    for h in range(2):
        own_k, own_v = mem_buf.at[h, a_own[h], 0], mem_buf.at[h, a_own[h], 1]
        go(mem_copy(h, 0, own_k, 1))
        go(mem_copy(h, 1, own_v, 3))
    for h in range(2):
        own_k, own_v = mem_buf.at[h, a_own[h], 0], mem_buf.at[h, a_own[h], 1]
        go(mem_copy(h, 2, own_v, 1))
        go(mem_copy(h, 3, own_k, 3))

    for h in range(2):
        kv_z_in(h).wait_recv()
    for d in (2, 1, 3):
        for h in range(2):
            go(kv_a(h, 1, d))
    for d in (1, 3, 2):
        for h in range(2):
            q_b_in(h, d).wait_recv()
            go(q_z(h, SIDE - d))
    for d in (1, 3, 2):
        for h in range(2):
            kv_a_in(h, 0, d).wait_recv()
            kv_a_in(h, 1, d).wait_recv()

    def local_shard(h, d):
        b = wrap(b_own[h] + d)
        if h == 0:
            tiles = x + jnp.where(y <= b, 1, 0)
            q_shard = (x * 4 + b) * 2 + z
        else:
            tiles = jnp.where(x < b, 4, jnp.where(x == b, y + 1, 0))
            q_shard = (b * 4 + y) * 2 + z
        lane_blk = lax.broadcasted_iota(jnp.int32, (1, 512), 1) // QBLK

        def block(blk, carry):
            tok = pl.ds(pl.multiple_of(blk * QBLK, QBLK), QBLK)
            q4 = q_buf[h, b, z, :, tok, :].reshape(SHARE * QBLK, DH)
            acc_ref[...] = jnp.zeros_like(acc_ref)
            max_ref[...] = jnp.full_like(max_ref, NEG)

            def tile(a, inner):
                k_shard = (a * 4 + y) * 2 if h == 0 else (x * 4 + a) * 2
                keys = kv_buf[h, a, 0].reshape(512, DH)
                vals = kv_buf[h, a, 1].reshape(512, DH)
                seen = k_shard * 2 + lane_blk <= q_shard * 2 + blk
                s = dot_nt(q4, keys) + jnp.where(seen, 0.0, NEG)
                old = max_ref[...]
                new = jnp.maximum(old, jnp.max(s, axis=1, keepdims=True))
                wide = jnp.concatenate([new] * 4, axis=1)
                p = jnp.exp2((s - wide) * FACTOR).astype(jnp.bfloat16)
                fade = jnp.exp2((old - new) * FACTOR)
                add = jnp.dot(p, with_ones(vals), preferred_element_type=jnp.float32)
                acc_ref[:, :DH] = acc_ref[:, :DH] * fade + add[:, :DH]
                acc_ref[:, DH:] = acc_ref[:, DH:] * fade + add[:, DH:]
                max_ref[...] = new
                return inner

            lax.fori_loop(0, tiles, tile, 0)
            total = acc_ref[:, DH:]
            some = total > 0.0
            safe = jnp.where(some, total, 1.0)
            result = acc_ref[:, :DH] / safe
            loc_part[h, b, :, tok, :] = result.astype(jnp.bfloat16).reshape(SHARE, QBLK, DH)
            lse = jnp.where(some, max_ref[...] * FACTOR + jnp.log2(safe), NEG)
            loc_lse[h, b, :, tok] = rows_of(lse)
            return carry

        lax.fori_loop(0, 2, block, 0)

    def loc_out(h, d):
        b = wrap(b_own[h] + d)
        return (
            remote(loc_part.at[h, b], loc_in.at[h, d], lo_s.at[h, d], lo_r.at[h, d], query_peer(h, d)),
            remote(loc_lse.at[h, b], loc_lse_in.at[h, d], ls_s.at[h, d], ls_r.at[h, d], query_peer(h, d)),
        )

    for d in (2, 1, 3, 0):
        for h in range(2):
            local_shard(h, d)
            if d:
                for cp in loc_out(h, d):
                    go(cp)
        if d == 2:
            for h in range(2):
                left, right = wrap(a_own[h] - 1), wrap(a_own[h] + 1)
                mem_copy(h, 0, mem_buf.at[h, left, 0], 1).wait_recv()
                go(mem_copy(h, 4, mem_buf.at[h, left, 0], 1))
                mem_copy(h, 1, mem_buf.at[h, right, 1], 3).wait_recv()
                go(mem_copy(h, 5, mem_buf.at[h, right, 1], 3))

    for h in range(2):
        for d in range(SIDE):
            for dz in range(2):
                if d or dz:
                    tab_in(h, d, dz).wait_recv()
    to_smem = pltpu.make_async_copy(tab_buf, tab_sm, l_sem.at[count])
    to_smem.start()
    to_smem.wait()
    for h in range(2):
        left, right = wrap(a_own[h] - 1), wrap(a_own[h] + 1)
        across = wrap(a_own[h] + 2)
        mem_copy(h, 2, mem_buf.at[h, left, 1], 1).wait_recv()
        mem_copy(h, 3, mem_buf.at[h, right, 0], 3).wait_recv()
        mem_copy(h, 4, mem_buf.at[h, across, 0], 1).wait_recv()
        mem_copy(h, 5, mem_buf.at[h, across, 1], 3).wait_recv()
        for d in range(SIDE):
            q_z_in(h, d).wait_recv()

    lane = lax.broadcasted_iota(jnp.int32, (1, 2 * MBLK), 1)

    def memory_shard(h, b, pz):
        def block(blk, carry):
            tok = pl.ds(pl.multiple_of(blk * QBLK, QBLK), QBLK)
            q4 = q_buf[h, b, pz, :, tok, :].reshape(SHARE * QBLK, DH)
            keys, vals, bias = [], [], []
            for a in range(SIDE):
                shard = (a * 4 + y) * 2 + z if h == 0 else (x * 4 + a) * 2 + z
                slots = [tab_sm[h, b, pz, blk, shard * 2 + k] for k in range(2)]
                for slot in slots:
                    at = jnp.maximum(slot, 0)
                    keys.append(mem_buf[h, a, 0, at])
                    vals.append(mem_buf[h, a, 1, at])
                off = [jnp.where(slot < 0, NEG, 0.0) for slot in slots]
                bias.append(jnp.where(lane < MBLK, off[0], off[1]))
            s = dot_nt(q4, jnp.concatenate(keys, axis=0)) + jnp.concatenate(bias, axis=1)
            top = jnp.max(s, axis=1, keepdims=True)
            p = jnp.exp2((s - top) * FACTOR).astype(jnp.bfloat16)
            both = jnp.dot(
                p, with_ones(jnp.concatenate(vals, axis=0)), preferred_element_type=jnp.float32
            )
            total = both[:, DH:]
            result = both[:, :DH] / total
            mem_part[h, b, pz, :, tok, :] = result.astype(jnp.bfloat16).reshape(SHARE, QBLK, DH)
            mem_lse[h, b, pz, :, tok] = rows_of(top * FACTOR + jnp.log2(total))
            return carry

        lax.fori_loop(0, 2, block, 0)

    def mem_out(h, part, d):
        b, pz = wrap(b_own[h] + d), (zo, z)[part]
        return (
            remote(mem_part.at[h, b, pz], mem_in.at[h, part, d], me_s.at[h, part, d], me_r.at[h, part, d], query_peer(h, d)),
            remote(mem_lse.at[h, b, pz], mem_lse_in.at[h, part, d], ms_s.at[h, part, d], ms_r.at[h, part, d], query_peer(h, d)),
        )

    def weights(stats):
        top = functools.reduce(jnp.maximum, stats)
        powers = [jnp.exp2(s - top) for s in stats]
        total = functools.reduce(jnp.add, powers)
        scales = [jnp.transpose(p / total) for p in powers]
        return scales, top + jnp.log2(total)

    def merge(parts, scales, g):
        total = None
        for part, scale in zip(parts, scales):
            term = part(g).astype(jnp.float32) * scale[:, g : g + 1]
            total = term if total is None else total + term
        return total

    for part in range(2):
        pz = (zo, z)[part]
        for d in (2, 1, 3, 0):
            for h in range(2):
                memory_shard(h, wrap(b_own[h] + d), pz)
                if d:
                    for cp in mem_out(h, part, d):
                        go(cp)

    for h in range(2):
        for d in range(1, SIDE):
            for cp in loc_out(h, d):
                cp.wait_recv()
        stats = [loc_lse[h, b_own[h]]] + [loc_lse_in[h, d] for d in range(1, SIDE)]
        scales, _ = weights(stats)
        parts = [lambda g, h=h: loc_part[h, b_own[h], g]]
        parts += [lambda g, h=h, d=d: loc_in[h, d, g] for d in range(1, SIDE)]
        for g in range(SHARE):
            loc_fin[h * SHARE + g] = merge(parts, scales, g)

    for part in range(2):
        pz = (zo, z)[part]
        for h in range(2):
            for d in range(1, SIDE):
                for cp in mem_out(h, part, d):
                    cp.wait_recv()
            stats = [mem_lse[h, b_own[h], pz]]
            stats += [mem_lse_in[h, part, d] for d in range(1, SIDE)]
            parts = [lambda g, h=h, pz=pz: mem_part[h, b_own[h], pz, g]]
            parts += [lambda g, h=h, d=d, part=part: mem_in[h, part, d, g] for d in range(1, SIDE)]
            z_data = remote(z_part.at[h], z_in.at[h], z_s.at[h], z_r.at[h], z_peer)
            z_stat = remote(z_lse.at[h], z_lse_in.at[h], zs_s.at[h], zs_r.at[h], z_peer)
            if part == 1:
                z_data.wait_recv()
                z_stat.wait_recv()
                stats.append(z_lse_in[h])
                parts.append(lambda g, h=h: z_in[h, g])
            scales, whole = weights(stats)
            for g in range(SHARE):
                result = merge(parts, scales, g)
                if part == 0:
                    z_part[h, g] = result.astype(jnp.bfloat16)
                else:
                    mem_fin[h * SHARE + g] = result
            if part == 0:
                z_lse[h] = whole
                go(z_data)
                go(z_stat)

    logits = jnp.zeros((ROWS, GROUPS * HEADS_DEV), jnp.float32)
    for head in range(HEADS_DEV):
        feats = pl.ds(head * DH, DH)
        logits += jnp.dot(
            loc_fin[head].astype(jnp.bfloat16), gw_ref[0, feats, :], preferred_element_type=jnp.float32
        )
        logits += jnp.dot(
            mem_fin[head].astype(jnp.bfloat16), gw_ref[1, feats, :], preferred_element_type=jnp.float32
        )
    lg_out[...] = jnp.transpose(logits).reshape(GROUPS, HEADS_DEV, ROWS)

    def lg(d):
        to = lax.rem(g_own + d, GROUPS)
        return remote(lg_out.at[to], lg_in.at[d], lg_s.at[d], lg_r.at[d], (c, to))

    for d in range(1, GROUPS):
        go(lg(d))
    own = lg_out[g_own]
    for d in range(1, GROUPS):
        lg(d).wait_recv()
        own = own + lg_in[d]
    gate = jax.nn.sigmoid(jnp.transpose(own) + gb_ref[...])
    for head in range(HEADS_DEV):
        share = gate[:, head : head + 1]
        mixed = share * mem_fin[head] + (1.0 - share) * loc_fin[head]
        out_ref[:, head * DH : (head + 1) * DH] = mixed.astype(jnp.bfloat16)

    for cp in started:
        cp.wait_send()


def block_table(retrieval):
    ids = retrieval.reshape(2, -1)
    owner, offset = ids // SHARD_BLOCKS, ids % SHARD_BLOCKS
    here = owner[:, None, :] == jnp.arange(32, dtype=jnp.int32)[None, :, None]
    held = jnp.sum(here.astype(jnp.int32), axis=2)
    low = jnp.min(jnp.where(here, offset[:, None, :], SHARD_BLOCKS), axis=2)
    high = jnp.max(jnp.where(here, offset[:, None, :], -1), axis=2)
    first = jnp.where(held > 0, low, -1)
    second = jnp.where(held > 1, high, -1)
    both = jnp.stack([first, second], axis=2).reshape(2, 64)
    return jnp.pad(both, ((0, 6), (0, 64)))


def on_device(queries, keys, values, mem_keys, mem_values, retrieval, gate_weight, gate_bias):
    bf, f32 = jnp.bfloat16, jnp.float32
    dma = pltpu.SemaphoreType.DMA
    anywhere = pl.BlockSpec(memory_space=pl.ANY)
    vmem = pl.BlockSpec(memory_space=pltpu.VMEM)
    part = (SHARE, ROWS, DH)
    stat = (8, ROWS)
    return pl.pallas_call(
        kernel,
        out_shape=jax.ShapeDtypeStruct((ROWS, HEADS_DEV * DH), bf),
        in_specs=[anywhere] * 6 + [vmem] * 2,
        out_specs=vmem,
        scratch_shapes=[
            pltpu.VMEM((2, SIDE, 2) + part, bf),
            pltpu.VMEM((2, SIDE, 2, 2, ROWS, DH), bf),
            pltpu.VMEM((2, SIDE, 2, SHARD_BLOCKS, MBLK, DH), bf),
            pltpu.VMEM((2, SIDE, 2, 8, 128), jnp.int32),
            pltpu.SMEM((2, SIDE, 2, 8, 128), jnp.int32),
            pltpu.VMEM((2, SIDE) + part, bf),
            pltpu.VMEM((2, SIDE) + stat, f32),
            pltpu.VMEM((2, SIDE) + part, bf),
            pltpu.VMEM((2, SIDE) + stat, f32),
            pltpu.VMEM((2, SIDE, 2) + part, bf),
            pltpu.VMEM((2, SIDE, 2) + stat, f32),
            pltpu.VMEM((2, 2, SIDE) + part, bf),
            pltpu.VMEM((2, 2, SIDE) + stat, f32),
            pltpu.VMEM((2,) + part, bf),
            pltpu.VMEM((2,) + stat, f32),
            pltpu.VMEM((2,) + part, bf),
            pltpu.VMEM((2,) + stat, f32),
            pltpu.VMEM((HEADS_DEV, ROWS, DH), f32),
            pltpu.VMEM((HEADS_DEV, ROWS, DH), f32),
            pltpu.VMEM((SHARE * QBLK, 2 * DH), f32),
            pltpu.VMEM((SHARE * QBLK, DH), f32),
            pltpu.VMEM((GROUPS, HEADS_DEV, ROWS), f32),
            pltpu.VMEM((GROUPS, HEADS_DEV, ROWS), f32),
            dma((24,)),
            dma((2,)), dma((2,)),
            dma((2, 2, SIDE)), dma((2, 2, SIDE)),
            dma((2, SIDE)), dma((2, SIDE)),
            dma((2, SIDE)), dma((2, SIDE)),
            dma((2, 8)), dma((2, 8)),
            dma((2, 6)), dma((2, 6)),
            dma((2, SIDE)), dma((2, SIDE)),
            dma((2, SIDE)), dma((2, SIDE)),
            dma((2, 2, SIDE)), dma((2, 2, SIDE)),
            dma((2, 2, SIDE)), dma((2, 2, SIDE)),
            dma((2,)), dma((2,)),
            dma((2,)), dma((2,)),
            dma((SIDE,)), dma((SIDE,)),
        ],
        compiler_params=pltpu.CompilerParams(
            collective_id=0, has_side_effects=True, vmem_limit_bytes=60 * 2**20
        ),
    )(
        queries, keys, values, mem_keys, mem_values, block_table(retrieval),
        gate_weight, gate_bias.reshape(1, HEADS_DEV),
    )


def solution(mesh):
    placed = (
        P("ctx", "mem"),
        P("ctx", "mem"),
        P("ctx", "mem"),
        P("ctx", None, "mem"),
        P("ctx", None, "mem"),
        P("ctx", "mem", None),
        P(None, "mem", None),
        P("mem"),
    )
    return jax.shard_map(
        on_device, mesh=mesh, in_specs=placed, out_specs=P("ctx", "mem"), check_vma=False
    )
```

```python
import functools
import math

import jax
import jax.numpy as jnp
from jax import lax
from jax.experimental import pallas as pl
from jax.experimental.pallas import tpu as pltpu
from jax.sharding import PartitionSpec as P

MESH = pl.DeviceIdType.MESH
SIDE = 4
DH = 128
SHARE = 4
QBLK = 128
ROWS = 256
SHARD_BLOCKS = 32
MBLK = 64
GROUPS = 4
HEADS_DEV = 8
NEG = -1e30
FACTOR = DH**-0.5 * math.log2(math.e)


def dot_nt(a, b):
    return lax.dot_general(a, b, (((1,), (1,)), ((), ())), preferred_element_type=jnp.float32)


def with_ones(v):
    return jnp.concatenate([v, jnp.ones_like(v)], axis=1)


def rows_of(pieces):
    shape = (QBLK, QBLK)
    eye = lax.broadcasted_iota(jnp.int32, shape, 0) == lax.broadcasted_iota(jnp.int32, shape, 1)
    rows = [jnp.sum(jnp.where(eye, piece, 0.0), axis=0, keepdims=True) for piece in pieces]
    return jnp.concatenate(rows + [jnp.zeros((8 - SHARE, QBLK), jnp.float32)], axis=0)


def block_table(ids):
    shape = (SHARD_BLOCKS, SHARD_BLOCKS)
    shard = lax.broadcasted_iota(jnp.int32, shape, 0)
    lane = lax.broadcasted_iota(jnp.int32, (SHARD_BLOCKS, 128), 1)
    table = jnp.full((SHARD_BLOCKS, 128), -1, jnp.int32)
    for l in range(2):
        row = ids[l : l + 1, :]
        held = row // SHARD_BLOCKS == shard
        offset = row % SHARD_BLOCKS + jnp.zeros_like(shard)
        low = jnp.min(jnp.where(held, offset, 99), axis=1, keepdims=True)
        high = jnp.max(jnp.where(held, offset, -1), axis=1, keepdims=True)
        first = jnp.where(low > 90, -1, low)
        second = jnp.where(high > low, high, -1)
        table = jnp.where(lane == 2 * l, first, jnp.where(lane == 2 * l + 1, second, table))
    turned = jnp.transpose(table)[:8]
    return jnp.concatenate([turned, jnp.full((8, 96), -1, jnp.int32)], axis=1)


def kernel(
    q_hbm, k_hbm, v_hbm, mk_hbm, mv_hbm, ids_ref, gw_ref, gb_ref,
    out_ref,
    q_buf, kv_buf, mem_buf, tab_buf, tab_sm,
    loc_part, loc_lse, loc_in, loc_lse_in,
    mem_part, mem_lse, mem_in, mem_lse_in,
    z_part, z_lse, z_in, z_lse_in,
    loc_fin, mem_fin, acc_ref, max_ref, lg_out, lg_in,
    l_sem, kvz_s, kvz_r, kva_s, kva_r, qb_s, qb_r, qz_s, qz_r, tab_s, tab_r, ma_s, ma_r,
    lo_s, lo_r, ls_s, ls_r, me_s, me_r, ms_s, ms_r, z_s, z_r, zs_s, zs_r, lg_s, lg_r,
):
    c = lax.axis_index("ctx")
    g_own = lax.axis_index("mem")
    x, y, z = c // 8, (c // 2) % 4, c % 2
    zo = 1 - z

    def wrap(i):
        return lax.rem(i + SIDE, SIDE)

    def device(px, py, pz):
        return (px * 8 + py * 2 + pz, g_own)

    def key_peer(h, d):
        return device(wrap(x + d), y, z) if h == 0 else device(x, wrap(y + d), z)

    def query_peer(h, d):
        return key_peer(1 - h, d)

    z_peer = device(x, y, zo)
    a_own = (x, y)
    b_own = (y, x)

    def remote(src, dst, ssem, rsem, peer):
        return pltpu.make_async_remote_copy(
            src_ref=src, dst_ref=dst, send_sem=ssem, recv_sem=rsem,
            device_id=peer, device_id_type=MESH,
        )

    kv_local, q_local, mem_local = [], [], []
    count = 0

    def local(src, dst, group):
        nonlocal count
        cp = pltpu.make_async_copy(src, dst, l_sem.at[count])
        cp.start()
        group.append(cp)
        count += 1

    for h in range(2):
        cols = pl.ds(h * DH, DH)
        local(k_hbm.at[:, cols], kv_buf.at[h, a_own[h], 0, z], kv_local)
        local(v_hbm.at[:, cols], kv_buf.at[h, a_own[h], 1, z], kv_local)
    for h in range(2):
        for g in range(SHARE):
            local(
                q_hbm.at[:, pl.ds((h * SHARE + g) * DH, DH)],
                q_buf.at[h, b_own[h], z, g],
                q_local,
            )
    for h in range(2):
        cols = pl.ds(h * DH, DH)
        local(mk_hbm.at[:, :, cols], mem_buf.at[h, a_own[h], 0], mem_local)
        local(mv_hbm.at[:, :, cols], mem_buf.at[h, a_own[h], 1], mem_local)

    barrier = pltpu.get_barrier_semaphore()
    greeted = [z_peer]
    for d in range(1, SIDE):
        greeted += [device(wrap(x + d), y, z), device(x, wrap(y + d), z)]
        greeted += [device(wrap(x + d), y, zo), device(x, wrap(y + d), zo)]
        greeted += [(c, lax.rem(g_own + d, GROUPS))]
    for peer in greeted:
        pl.semaphore_signal(barrier, inc=1, device_id=peer, device_id_type=MESH)
    pl.semaphore_wait(barrier, len(greeted))

    started = []

    def go(cp):
        cp.start()
        started.append(cp)
        return cp

    def kv_z(h):
        ref = kv_buf.at[h, a_own[h], :, z]
        return remote(ref, ref, kvz_s.at[h], kvz_r.at[h], z_peer)

    def kv_z_in(h):
        ref = kv_buf.at[h, a_own[h], :, zo]
        return remote(ref, ref, kvz_s.at[h], kvz_r.at[h], z_peer)

    def ring(h, own, peer, ref, ssem, rsem):
        left, right, across = wrap(own - 1), wrap(own + 1), wrap(own + 2)
        out = [(own, 0, 1), (own, 1, 3), (own, 1, 1), (own, 0, 3), (left, 0, 1), (right, 1, 3)]
        come = [(left, 0), (right, 1), (left, 1), (right, 0), (across, 0), (across, 1)]

        def send(n):
            at, half, d = out[n]
            go(remote(ref(at, half), ref(at, half), ssem.at[n], rsem.at[n], peer(h, d)))

        def wait(n):
            at, half = come[n]
            remote(ref(at, half), ref(at, half), ssem.at[n], rsem.at[n], z_peer).wait_recv()

        return send, wait

    def kv_ring(h, part):
        pz = (z, zo)[part]
        return ring(
            h, a_own[h], key_peer, lambda at, half: kv_buf.at[h, at, half, pz],
            kva_s.at[h, part], kva_r.at[h, part],
        )

    def q_ring(h):
        return ring(
            h, b_own[h], query_peer, lambda at, half: q_buf.at[h, at, z, pl.ds(2 * half, 2)],
            qb_s.at[h], qb_r.at[h],
        )

    def mem_ring(h):
        return ring(
            h, a_own[h], key_peer, lambda at, half: mem_buf.at[h, at, half], ma_s.at[h], ma_r.at[h]
        )

    def q_z(h, d):
        ref = q_buf.at[h, wrap(b_own[h] + d), z]
        return remote(ref, ref, qz_s.at[h, d], qz_r.at[h, d], z_peer)

    def q_z_in(h, d):
        ref = q_buf.at[h, wrap(b_own[h] + d), zo]
        return remote(ref, ref, qz_s.at[h, d], qz_r.at[h, d], z_peer)

    def tab_peer(h, d, dz):
        pz = zo if dz else z
        return device(x, wrap(y + d), pz) if h == 0 else device(wrap(x + d), y, pz)

    def tab(h, d, dz):
        ref = tab_buf.at[h, b_own[h], z]
        sem = d * 2 + dz
        return remote(ref, ref, tab_s.at[h, sem], tab_r.at[h, sem], tab_peer(h, d, dz))

    def tab_in(h, d, dz):
        ref = tab_buf.at[h, wrap(b_own[h] - d), zo if dz else z]
        sem = d * 2 + dz
        return remote(ref, ref, tab_s.at[h, sem], tab_r.at[h, sem], tab_peer(h, d, dz))

    q_rings = [q_ring(h) for h in range(2)]
    kv_rings = [kv_ring(h, 0) for h in range(2)]
    kvo_rings = [kv_ring(h, 1) for h in range(2)]
    mem_rings = [mem_ring(h) for h in range(2)]

    def on(rings, what, *steps):
        for n in steps:
            for r in rings:
                r[what](n)

    SEND, WAIT = 0, 1
    for cp in kv_local:
        cp.wait()
    for h in range(2):
        go(kv_z(h))
    for cp in q_local:
        cp.wait()
    on(q_rings, SEND, 0, 1)
    on(kv_rings, SEND, 0, 1)
    on(q_rings, SEND, 2, 3)
    on(kv_rings, SEND, 2, 3)
    for h in range(2):
        go(q_z(h, 0))
    for cp in mem_local:
        cp.wait()
    on(mem_rings, SEND, 0, 1)
    for h in range(2):
        tab_buf[h, b_own[h], z] = block_table(ids_ref[...])
    for h in range(2):
        for d in range(SIDE):
            for dz in range(2):
                if d or dz:
                    go(tab(h, d, dz))

    on(q_rings, WAIT, 0, 1)
    on(q_rings, SEND, 4, 5)
    on(kv_rings, WAIT, 0, 1)
    on(kv_rings, SEND, 4, 5)
    for h in range(2):
        kv_z_in(h).wait_recv()
    on(kvo_rings, SEND, 0, 1, 2, 3)
    on(mem_rings, SEND, 2, 3)
    on(q_rings, WAIT, 2, 3)
    for h in range(2):
        go(q_z(h, 1))
        go(q_z(h, 3))
    on(kvo_rings, WAIT, 0, 1)
    on(kvo_rings, SEND, 4, 5)
    on(q_rings, WAIT, 4, 5)
    for h in range(2):
        go(q_z(h, 2))
    on(kv_rings, WAIT, 2, 3, 4, 5)
    on(kvo_rings, WAIT, 2, 3, 4, 5)

    def local_shard(h, d):
        b = wrap(b_own[h] + d)
        if h == 0:
            tiles = x + jnp.where(y <= b, 1, 0)
            q_shard = (x * 4 + b) * 2 + z
        else:
            tiles = jnp.where(x < b, 4, jnp.where(x == b, y + 1, 0))
            q_shard = (b * 4 + y) * 2 + z
        lane_blk = lax.broadcasted_iota(jnp.int32, (1, 512), 1) // QBLK

        acc_ref[...] = jnp.zeros_like(acc_ref)
        max_ref[...] = jnp.full_like(max_ref, NEG)

        def tile(a, carry):
            k_shard = (a * 4 + y) * 2 if h == 0 else (x * 4 + a) * 2
            keys = kv_buf[h, a, 0].reshape(512, DH)
            vals = with_ones(kv_buf[h, a, 1].reshape(512, DH))
            for blk in range(2):
                seen = k_shard * 2 + lane_blk <= q_shard * 2 + blk
                bias = jnp.where(seen, 0.0, NEG)
                for g in range(SHARE):
                    n = blk * SHARE + g
                    q = q_buf[h, b, z, g, blk * QBLK : (blk + 1) * QBLK, :]
                    s = dot_nt(q, keys) + bias
                    old = max_ref[n]
                    new = jnp.maximum(old, jnp.max(s, axis=1, keepdims=True))
                    wide = jnp.concatenate([new] * 4, axis=1)
                    p = jnp.exp2((s - wide) * FACTOR).astype(jnp.bfloat16)
                    fade = jnp.exp2((old - new) * FACTOR)
                    add = jnp.dot(p, vals, preferred_element_type=jnp.float32)
                    acc_ref[n, :, :DH] = acc_ref[n, :, :DH] * fade + add[:, :DH]
                    acc_ref[n, :, DH:] = acc_ref[n, :, DH:] * fade + add[:, DH:]
                    max_ref[n] = new
            return carry

        lax.fori_loop(0, tiles, tile, 0)
        for blk in range(2):
            tok = slice(blk * QBLK, (blk + 1) * QBLK)
            sums = []
            for g in range(SHARE):
                n = blk * SHARE + g
                total = acc_ref[n, :, DH:]
                some = total > 0.0
                safe = jnp.where(some, total, 1.0)
                loc_part[h, b, g, tok, :] = (acc_ref[n, :, :DH] / safe).astype(jnp.bfloat16)
                sums.append(jnp.where(some, max_ref[n] * FACTOR + jnp.log2(safe), NEG))
            loc_lse[h, b, :, tok] = rows_of(sums)

    def loc_out(h, d):
        b = wrap(b_own[h] + d)
        return (
            remote(loc_part.at[h, b], loc_in.at[h, d], lo_s.at[h, d], lo_r.at[h, d], query_peer(h, d)),
            remote(loc_lse.at[h, b], loc_lse_in.at[h, d], ls_s.at[h, d], ls_r.at[h, d], query_peer(h, d)),
        )

    def local_step(i, carry):
        d = lax.rem(i + 1, SIDE)
        for h in range(2):
            local_shard(h, d)

        @pl.when(d != 0)
        def _():
            for h in range(2):
                for cp in loc_out(h, d):
                    cp.start()

        return carry

    lax.fori_loop(0, 1, local_step, 0)
    on(mem_rings, WAIT, 0, 1)
    on(mem_rings, SEND, 4, 5)
    lax.fori_loop(1, SIDE, local_step, 0)

    for h in range(2):
        for d in range(SIDE):
            for dz in range(2):
                if d or dz:
                    tab_in(h, d, dz).wait_recv()
    to_smem = pltpu.make_async_copy(tab_buf, tab_sm, l_sem.at[count])
    to_smem.start()
    to_smem.wait()
    on(mem_rings, WAIT, 2, 3, 4, 5)
    for h in range(2):
        for d in range(SIDE):
            q_z_in(h, d).wait_recv()

    lane = lax.broadcasted_iota(jnp.int32, (1, 2 * MBLK), 1)

    def memory_shard(h, b, pz):
        for blk in range(2):
            tok = slice(blk * QBLK, (blk + 1) * QBLK)
            keys, vals, bias = [], [], []
            for a in range(SIDE):
                shard = (a * 4 + y) * 2 + z if h == 0 else (x * 4 + a) * 2 + z
                slots = [tab_sm[h, b, pz, 2 * blk + k, shard] for k in range(2)]
                for slot in slots:
                    at = jnp.clip(slot, 0, SHARD_BLOCKS - 1)
                    keys.append(mem_buf[h, a, 0, at])
                    vals.append(mem_buf[h, a, 1, at])
                off = [jnp.where(slot < 0, NEG, 0.0) for slot in slots]
                bias.append(jnp.where(lane < MBLK, off[0], off[1]))
            keys = jnp.concatenate(keys, axis=0)
            vals = with_ones(jnp.concatenate(vals, axis=0))
            bias = jnp.concatenate(bias, axis=1)
            sums = []
            for g in range(SHARE):
                s = dot_nt(q_buf[h, b, pz, g, tok, :], keys) + bias
                top = jnp.max(s, axis=1, keepdims=True)
                p = jnp.exp2((s - top) * FACTOR).astype(jnp.bfloat16)
                both = jnp.dot(p, vals, preferred_element_type=jnp.float32)
                total = both[:, DH:]
                mem_part[h, b, pz, g, tok, :] = (both[:, :DH] / total).astype(jnp.bfloat16)
                sums.append(top * FACTOR + jnp.log2(total))
            mem_lse[h, b, pz, :, tok] = rows_of(sums)

    def mem_out(h, part, d):
        b, pz = wrap(b_own[h] + d), (zo, z)[part]
        return (
            remote(mem_part.at[h, b, pz], mem_in.at[h, part, d], me_s.at[h, part, d], me_r.at[h, part, d], query_peer(h, d)),
            remote(mem_lse.at[h, b, pz], mem_lse_in.at[h, part, d], ms_s.at[h, part, d], ms_r.at[h, part, d], query_peer(h, d)),
        )

    def weights(stats):
        top = functools.reduce(jnp.maximum, stats)
        powers = [jnp.exp2(s - top) for s in stats]
        total = functools.reduce(jnp.add, powers)
        scales = [jnp.transpose(p / total) for p in powers]
        return scales, top + jnp.log2(total)

    def merge(parts, scales, g):
        total = None
        for part, scale in zip(parts, scales):
            term = part(g).astype(jnp.float32) * scale[:, g : g + 1]
            total = term if total is None else total + term
        return total

    for part in range(2):

        def memory_step(i, carry, part=part):
            d = lax.rem(i + 1, SIDE)
            for h in range(2):
                memory_shard(h, wrap(b_own[h] + d), (zo, z)[part])

            @pl.when(d != 0)
            def _():
                for h in range(2):
                    for cp in mem_out(h, part, d):
                        cp.start()

            return carry

        lax.fori_loop(0, SIDE, memory_step, 0)

    for h in range(2):
        for d in range(1, SIDE):
            for cp in loc_out(h, d):
                cp.wait_recv()
        stats = [loc_lse[h, b_own[h]]] + [loc_lse_in[h, d] for d in range(1, SIDE)]
        scales, _ = weights(stats)
        parts = [lambda g, h=h: loc_part[h, b_own[h], g]]
        parts += [lambda g, h=h, d=d: loc_in[h, d, g] for d in range(1, SIDE)]
        for g in range(SHARE):
            loc_fin[h * SHARE + g] = merge(parts, scales, g)

    for part in range(2):
        pz = (zo, z)[part]
        for h in range(2):
            for d in range(1, SIDE):
                for cp in mem_out(h, part, d):
                    cp.wait_recv()
            stats = [mem_lse[h, b_own[h], pz]]
            stats += [mem_lse_in[h, part, d] for d in range(1, SIDE)]
            parts = [lambda g, h=h, pz=pz: mem_part[h, b_own[h], pz, g]]
            parts += [lambda g, h=h, d=d, part=part: mem_in[h, part, d, g] for d in range(1, SIDE)]
            z_data = remote(z_part.at[h], z_in.at[h], z_s.at[h], z_r.at[h], z_peer)
            z_stat = remote(z_lse.at[h], z_lse_in.at[h], zs_s.at[h], zs_r.at[h], z_peer)
            if part == 1:
                z_data.wait_recv()
                z_stat.wait_recv()
                stats.append(z_lse_in[h])
                parts.append(lambda g, h=h: z_in[h, g])
            scales, whole = weights(stats)
            for g in range(SHARE):
                result = merge(parts, scales, g)
                if part == 0:
                    z_part[h, g] = result.astype(jnp.bfloat16)
                else:
                    mem_fin[h * SHARE + g] = result
            if part == 0:
                z_lse[h] = whole
                go(z_data)
                go(z_stat)

    logits = jnp.zeros((GROUPS * HEADS_DEV, ROWS), jnp.float32)
    for head in range(HEADS_DEV):
        feats = slice(head * DH, (head + 1) * DH)
        logits += dot_nt(gw_ref[0, :, feats], loc_fin[head].astype(jnp.bfloat16))
        logits += dot_nt(gw_ref[1, :, feats], mem_fin[head].astype(jnp.bfloat16))
    lg_out[...] = logits.reshape(GROUPS, HEADS_DEV, ROWS)

    def lg(d):
        to = lax.rem(g_own + d, GROUPS)
        return remote(lg_out.at[to], lg_in.at[d], lg_s.at[d], lg_r.at[d], (c, to))

    for d in range(1, GROUPS):
        go(lg(d))
    own = lg_out[g_own]
    for d in range(1, GROUPS):
        lg(d).wait_recv()
        own = own + lg_in[d]
    gate = jax.nn.sigmoid(jnp.transpose(own) + gb_ref[...])
    for head in range(HEADS_DEV):
        share = gate[:, head : head + 1]
        mixed = share * mem_fin[head] + (1.0 - share) * loc_fin[head]
        out_ref[:, head * DH : (head + 1) * DH] = mixed.astype(jnp.bfloat16)

    for h in range(2):
        for d in range(1, SIDE):
            for cp in loc_out(h, d) + mem_out(h, 0, d) + mem_out(h, 1, d):
                cp.wait_send()
    for cp in started:
        cp.wait_send()


def on_device(queries, keys, values, mem_keys, mem_values, retrieval, gate_weight, gate_bias):
    bf, f32 = jnp.bfloat16, jnp.float32
    dma = pltpu.SemaphoreType.DMA
    anywhere = pl.BlockSpec(memory_space=pl.ANY)
    vmem = pl.BlockSpec(memory_space=pltpu.VMEM)
    part = (SHARE, ROWS, DH)
    stat = (8, ROWS)
    return pl.pallas_call(
        kernel,
        out_shape=jax.ShapeDtypeStruct((ROWS, HEADS_DEV * DH), bf),
        in_specs=[anywhere] * 5 + [vmem] * 3,
        out_specs=vmem,
        scratch_shapes=[
            pltpu.VMEM((2, SIDE, 2) + part, bf),
            pltpu.VMEM((2, SIDE, 2, 2, ROWS, DH), bf),
            pltpu.VMEM((2, SIDE, 2, SHARD_BLOCKS, MBLK, DH), bf),
            pltpu.VMEM((2, SIDE, 2, 8, 128), jnp.int32),
            pltpu.SMEM((2, SIDE, 2, 8, 128), jnp.int32),
            pltpu.VMEM((2, SIDE) + part, bf),
            pltpu.VMEM((2, SIDE) + stat, f32),
            pltpu.VMEM((2, SIDE) + part, bf),
            pltpu.VMEM((2, SIDE) + stat, f32),
            pltpu.VMEM((2, SIDE, 2) + part, bf),
            pltpu.VMEM((2, SIDE, 2) + stat, f32),
            pltpu.VMEM((2, 2, SIDE) + part, bf),
            pltpu.VMEM((2, 2, SIDE) + stat, f32),
            pltpu.VMEM((2,) + part, bf),
            pltpu.VMEM((2,) + stat, f32),
            pltpu.VMEM((2,) + part, bf),
            pltpu.VMEM((2,) + stat, f32),
            pltpu.VMEM((HEADS_DEV, ROWS, DH), f32),
            pltpu.VMEM((HEADS_DEV, ROWS, DH), f32),
            pltpu.VMEM((2 * SHARE, QBLK, 2 * DH), f32),
            pltpu.VMEM((2 * SHARE, QBLK, DH), f32),
            pltpu.VMEM((GROUPS, HEADS_DEV, ROWS), f32),
            pltpu.VMEM((GROUPS, HEADS_DEV, ROWS), f32),
            dma((24,)),
            dma((2,)), dma((2,)),
            dma((2, 2, 6)), dma((2, 2, 6)),
            dma((2, 6)), dma((2, 6)),
            dma((2, SIDE)), dma((2, SIDE)),
            dma((2, 8)), dma((2, 8)),
            dma((2, 6)), dma((2, 6)),
            dma((2, SIDE)), dma((2, SIDE)),
            dma((2, SIDE)), dma((2, SIDE)),
            dma((2, 2, SIDE)), dma((2, 2, SIDE)),
            dma((2, 2, SIDE)), dma((2, 2, SIDE)),
            dma((2,)), dma((2,)),
            dma((2,)), dma((2,)),
            dma((SIDE,)), dma((SIDE,)),
        ],
        compiler_params=pltpu.CompilerParams(
            collective_id=0, has_side_effects=True, vmem_limit_bytes=60 * 2**20
        ),
    )(
        queries, keys, values, mem_keys, mem_values, retrieval.reshape(2, -1),
        gate_weight.transpose(0, 2, 1), gate_bias.reshape(1, HEADS_DEV),
    )


def solution(mesh):
    placed = (
        P("ctx", "mem"),
        P("ctx", "mem"),
        P("ctx", "mem"),
        P("ctx", None, "mem"),
        P("ctx", None, "mem"),
        P("ctx", "mem", None),
        P(None, "mem", None),
        P("mem"),
    )
    return jax.shard_map(
        on_device, mesh=mesh, in_specs=placed, out_specs=P("ctx", "mem"), check_vma=False
    )
```

```python
import functools
import math

import jax
import jax.numpy as jnp
from jax import lax
from jax.experimental import pallas as pl
from jax.experimental.pallas import tpu as pltpu
from jax.sharding import PartitionSpec as P

MESH = pl.DeviceIdType.MESH
SIDE = 4
DH = 128
SHARE = 4
QBLK = 128
ROWS = 256
SHARD_BLOCKS = 32
MBLK = 64
GROUPS = 4
HEADS_DEV = 8
NEG = -1e30
FACTOR = DH**-0.5 * math.log2(math.e)


def dot_nt(a, b):
    return lax.dot_general(a, b, (((1,), (1,)), ((), ())), preferred_element_type=jnp.float32)


def with_ones(v):
    return jnp.concatenate([v, jnp.ones_like(v)], axis=1)


def rows_of(pieces):
    shape = (QBLK, QBLK)
    eye = lax.broadcasted_iota(jnp.int32, shape, 0) == lax.broadcasted_iota(jnp.int32, shape, 1)
    rows = [jnp.sum(jnp.where(eye, piece, 0.0), axis=0, keepdims=True) for piece in pieces]
    return jnp.concatenate(rows + [jnp.zeros((6, QBLK), jnp.float32)], axis=0)


def block_table(ids):
    shape = (SHARD_BLOCKS, SHARD_BLOCKS)
    shard = lax.broadcasted_iota(jnp.int32, shape, 0)
    lane = lax.broadcasted_iota(jnp.int32, (SHARD_BLOCKS, 128), 1)
    table = jnp.full((SHARD_BLOCKS, 128), -1, jnp.int32)
    for l in range(2):
        row = ids[l : l + 1, :]
        held = row // SHARD_BLOCKS == shard
        offset = row % SHARD_BLOCKS + jnp.zeros_like(shard)
        low = jnp.min(jnp.where(held, offset, 99), axis=1, keepdims=True)
        high = jnp.max(jnp.where(held, offset, -1), axis=1, keepdims=True)
        first = jnp.where(low > 90, -1, low)
        second = jnp.where(high > low, high, -1)
        table = jnp.where(lane == 2 * l, first, jnp.where(lane == 2 * l + 1, second, table))
    turned = jnp.transpose(table)[:8]
    return jnp.concatenate([turned, jnp.full((8, 96), -1, jnp.int32)], axis=1)


def kernel(
    q_hbm, k_hbm, v_hbm, mk_hbm, mv_hbm, ids_ref, gw_ref, gb_ref,
    out_ref,
    q_buf, kv_buf, mem_buf, tab_buf, tab_sm,
    part_buf, lse_buf, in_buf, in_lse, z_part, z_lse, z_in, z_lse_in,
    loc_fin, mem_fin, acc_ref, max_ref, lg_out, lg_in,
    l_sem, kvz_s, kvz_r, kva_s, kva_r, qb_s, qb_r, qz_s, qz_r, tab_s, tab_r, ma_s, ma_r,
    rs_s, rs_r, rl_s, rl_r, z_s, z_r, zs_s, zs_r, lg_s, lg_r,
):
    c = lax.axis_index("ctx")
    g_own = lax.axis_index("mem")
    x, y, z = c // 8, (c // 2) % 4, c % 2
    zo = 1 - z

    def wrap(i):
        return lax.rem(i + SIDE, SIDE)

    def device(px, py, pz):
        return (px * 8 + py * 2 + pz, g_own)

    def key_peer(h, d):
        return device(wrap(x + d), y, z) if h == 0 else device(x, wrap(y + d), z)

    def query_peer(h, d):
        return key_peer(1 - h, d)

    z_peer = device(x, y, zo)
    a_own = (x, y)
    b_own = (y, x)

    def remote(src, dst, ssem, rsem, peer):
        return pltpu.make_async_remote_copy(
            src_ref=src, dst_ref=dst, send_sem=ssem, recv_sem=rsem,
            device_id=peer, device_id_type=MESH,
        )

    kv_local, q_local, mem_local = [], [], []
    count = 0

    def local(src, dst, group):
        nonlocal count
        cp = pltpu.make_async_copy(src, dst, l_sem.at[count])
        cp.start()
        group.append(cp)
        count += 1

    for h in range(2):
        cols = pl.ds(h * DH, DH)
        local(k_hbm.at[:, cols], kv_buf.at[h, a_own[h], 0, z], kv_local)
        local(v_hbm.at[:, cols], kv_buf.at[h, a_own[h], 1, z], kv_local)
    for h in range(2):
        for g in range(SHARE):
            local(
                q_hbm.at[:, pl.ds((h * SHARE + g) * DH, DH)],
                q_buf.at[h, b_own[h], z, g],
                q_local,
            )
    for h in range(2):
        cols = pl.ds(h * DH, DH)
        local(mk_hbm.at[:, :, cols], mem_buf.at[h, a_own[h], 0], mem_local)
        local(mv_hbm.at[:, :, cols], mem_buf.at[h, a_own[h], 1], mem_local)

    barrier = pltpu.get_barrier_semaphore()
    greeted = [z_peer]
    for d in range(1, SIDE):
        greeted += [device(wrap(x + d), y, z), device(x, wrap(y + d), z)]
        greeted += [device(wrap(x + d), y, zo), device(x, wrap(y + d), zo)]
        greeted += [(c, lax.rem(g_own + d, GROUPS))]
    for peer in greeted:
        pl.semaphore_signal(barrier, inc=1, device_id=peer, device_id_type=MESH)
    pl.semaphore_wait(barrier, len(greeted))

    started = []

    def go(cp):
        cp.start()
        started.append(cp)
        return cp

    def kv_z(h):
        ref = kv_buf.at[h, a_own[h], :, z]
        return remote(ref, ref, kvz_s.at[h], kvz_r.at[h], z_peer)

    def kv_z_in(h):
        ref = kv_buf.at[h, a_own[h], :, zo]
        return remote(ref, ref, kvz_s.at[h], kvz_r.at[h], z_peer)

    def ring(h, own, peer, ref, ssem, rsem):
        left, right, across = wrap(own - 1), wrap(own + 1), wrap(own + 2)
        out = [(own, 0, 1), (own, 1, 3), (own, 1, 1), (own, 0, 3), (left, 0, 1), (right, 1, 3)]
        come = [(left, 0), (right, 1), (left, 1), (right, 0), (across, 0), (across, 1)]

        def copy(n):
            at, half, d = out[n]
            return remote(ref(at, half), ref(at, half), ssem.at[n], rsem.at[n], peer(h, d))

        def send(n):
            copy(n).start()

        def sent(n):
            copy(n).wait_send()

        def wait(n):
            at, half = come[n]
            remote(ref(at, half), ref(at, half), ssem.at[n], rsem.at[n], z_peer).wait_recv()

        return send, wait, sent

    def kv_ring(h, part):
        pz = (z, zo)[part]
        return ring(
            h, a_own[h], key_peer, lambda at, half: kv_buf.at[h, at, half, pz],
            kva_s.at[h, part], kva_r.at[h, part],
        )

    def q_ring(h):
        return ring(
            h, b_own[h], query_peer, lambda at, half: q_buf.at[h, at, z, pl.ds(2 * half, 2)],
            qb_s.at[h], qb_r.at[h],
        )

    def mem_ring(h, part):
        blocks = pl.ds(part * (SHARD_BLOCKS // 2), SHARD_BLOCKS // 2)
        return ring(
            h, a_own[h], key_peer, lambda at, half: mem_buf.at[h, at, half, blocks],
            ma_s.at[h, part], ma_r.at[h, part],
        )

    def q_z(h, d):
        ref = q_buf.at[h, wrap(b_own[h] + d), z]
        return remote(ref, ref, qz_s.at[h, d], qz_r.at[h, d], z_peer)

    def q_z_in(h, d):
        ref = q_buf.at[h, wrap(b_own[h] + d), zo]
        return remote(ref, ref, qz_s.at[h, d], qz_r.at[h, d], z_peer)

    def tab_peer(h, d, dz):
        pz = zo if dz else z
        return device(x, wrap(y + d), pz) if h == 0 else device(wrap(x + d), y, pz)

    def tab(h, d, dz):
        ref = tab_buf.at[h, b_own[h], z]
        sem = d * 2 + dz
        return remote(ref, ref, tab_s.at[h, sem], tab_r.at[h, sem], tab_peer(h, d, dz))

    def tab_in(h, d, dz):
        ref = tab_buf.at[h, wrap(b_own[h] - d), zo if dz else z]
        sem = d * 2 + dz
        return remote(ref, ref, tab_s.at[h, sem], tab_r.at[h, sem], tab_peer(h, d, dz))

    q_rings = [q_ring(h) for h in range(2)]
    kv_rings = [kv_ring(h, 0) for h in range(2)]
    kvo_rings = [kv_ring(h, 1) for h in range(2)]
    mem_a_rings = [mem_ring(h, 0) for h in range(2)]
    mem_b_rings = [mem_ring(h, 1) for h in range(2)]

    def on(rings, what, *steps):
        for n in steps:
            for r in rings:
                r[what](n)

    SEND, WAIT, SENT = 0, 1, 2
    for cp in kv_local:
        cp.wait()
    for h in range(2):
        go(kv_z(h))
    for cp in q_local:
        cp.wait()
    on(q_rings, SEND, 0, 1)
    on(kv_rings, SEND, 0, 1)
    on(q_rings, SEND, 2, 3)
    on(kv_rings, SEND, 2, 3)
    for h in range(2):
        go(q_z(h, 0))
    for cp in mem_local:
        cp.wait()
    on(mem_a_rings, SEND, 0, 1)
    for h in range(2):
        kv_z_in(h).wait_recv()
    on(kvo_rings, SEND, 0, 1, 2, 3)
    on(q_rings, WAIT, 0, 1)
    on(q_rings, SEND, 4, 5)
    on(kv_rings, WAIT, 0, 1)
    on(kv_rings, SEND, 4, 5)
    on(mem_a_rings, SEND, 2, 3)
    on(q_rings, WAIT, 2, 3)
    for h in range(2):
        go(q_z(h, 1))
        go(q_z(h, 3))
    on(kvo_rings, WAIT, 0, 1)
    on(kvo_rings, SEND, 4, 5)
    on(mem_b_rings, SEND, 0, 1, 2, 3)
    for h in range(2):
        tab_buf[h, b_own[h], z] = block_table(ids_ref[...])
    for h in range(2):
        for d in range(SIDE):
            for dz in range(2):
                if d or dz:
                    go(tab(h, d, dz))
    on(q_rings, WAIT, 4, 5)
    for h in range(2):
        go(q_z(h, 2))
    on(kv_rings, WAIT, 2, 3, 4, 5)
    on(kvo_rings, WAIT, 2, 3, 4, 5)
    on(mem_a_rings, WAIT, 0, 1)
    on(mem_a_rings, SEND, 4, 5)

    def local_shard(h, d):
        b = wrap(b_own[h] + d)
        if h == 0:
            tiles = x + jnp.where(y <= b, 1, 0)
            q_shard = (x * 4 + b) * 2 + z
        else:
            tiles = jnp.where(x < b, 4, jnp.where(x == b, y + 1, 0))
            q_shard = (b * 4 + y) * 2 + z
        lane_blk = lax.broadcasted_iota(jnp.int32, (1, 512), 1) // QBLK

        acc_ref[...] = jnp.zeros_like(acc_ref)
        max_ref[...] = jnp.full_like(max_ref, NEG)

        def tile(a, carry):
            k_shard = (a * 4 + y) * 2 if h == 0 else (x * 4 + a) * 2
            keys = kv_buf[h, a, 0].reshape(512, DH)
            vals = with_ones(kv_buf[h, a, 1].reshape(512, DH))
            for blk in range(2):
                seen = k_shard * 2 + lane_blk <= q_shard * 2 + blk
                bias = jnp.where(seen, 0.0, NEG)
                for g in range(SHARE):
                    n = blk * SHARE + g
                    q = q_buf[h, b, z, g, blk * QBLK : (blk + 1) * QBLK, :]
                    s = dot_nt(q, keys) + bias
                    old = max_ref[n]
                    new = jnp.maximum(old, jnp.max(s, axis=1, keepdims=True))
                    wide = jnp.concatenate([new] * 4, axis=1)
                    p = jnp.exp2((s - wide) * FACTOR).astype(jnp.bfloat16)
                    fade = jnp.exp2((old - new) * FACTOR)
                    add = jnp.dot(p, vals, preferred_element_type=jnp.float32)
                    acc_ref[n, :, :DH] = acc_ref[n, :, :DH] * fade + add[:, :DH]
                    acc_ref[n, :, DH:] = acc_ref[n, :, DH:] * fade + add[:, DH:]
                    max_ref[n] = new
            return carry

        lax.fori_loop(0, tiles, tile, 0)
        for blk in range(2):
            tok = slice(blk * QBLK, (blk + 1) * QBLK)
            sums = []
            for g in range(SHARE):
                n = blk * SHARE + g
                total = acc_ref[n, :, DH:]
                some = total > 0.0
                safe = jnp.where(some, total, 1.0)
                part_buf[0, h, b, g, tok, :] = (acc_ref[n, :, :DH] / safe).astype(jnp.bfloat16)
                sums.append(jnp.where(some, max_ref[n] * FACTOR + jnp.log2(safe), NEG))
            lse_buf[0, h, b, 0, :, tok] = rows_of(sums[:2])
            lse_buf[0, h, b, 1, :, tok] = rows_of(sums[2:])

    MESSAGES = [(2, 0, 1, 0), (2, 1, 3, 0), (1, 1, 1, 1), (3, 0, 3, 2), (1, 0, 1, 1), (3, 1, 3, 2)]

    def result_copies(job, h, n):
        whose, half, way, lands = MESSAGES[n]
        b = wrap(b_own[h] + whose)
        heads = pl.ds(2 * half, 2)
        peer = query_peer(h, way)
        return (
            remote(
                part_buf.at[job, h, b, heads], in_buf.at[job, h, lands, heads],
                rs_s.at[job, h, n], rs_r.at[job, h, n], peer,
            ),
            remote(
                lse_buf.at[job, h, b, half], in_lse.at[job, h, lands, half],
                rl_s.at[job, h, n], rl_r.at[job, h, n], peer,
            ),
        )

    def send_results(job, *numbers, hs=(0, 1)):
        for n in numbers:
            for h in hs:
                for cp in result_copies(job, h, n):
                    cp.start()

    def await_results(job, *numbers, hs=(0, 1)):
        for n in numbers:
            for h in hs:
                for cp in result_copies(job, h, n):
                    cp.wait_recv()

    def weights(stats):
        top = functools.reduce(jnp.maximum, stats)
        powers = [jnp.exp2(s - top) for s in stats]
        total = functools.reduce(jnp.add, powers)
        scales = [jnp.transpose(p / total) for p in powers]
        return scales, top + jnp.log2(total)

    def merge(parts, scales, g):
        total = None
        for part, scale in zip(parts, scales):
            term = part[g].astype(jnp.float32) * scale[:, g % 2 : g % 2 + 1]
            total = term if total is None else total + term
        return total

    def pass_on(job):
        for half in range(2):
            for h in range(2):
                await_results(job, half, hs=(h,))
                b = wrap(b_own[h] + (1, 3)[half])
                mine, other = part_buf.at[job, h, b], in_buf.at[job, h, 0]
                scales, whole = weights([lse_buf[job, h, b, half], in_lse[job, h, 0, half]])
                for g in (2 * half, 2 * half + 1):
                    mine[g] = merge([mine, other], scales, g).astype(jnp.bfloat16)
                lse_buf[job, h, b, half] = whole
                send_results(job, 4 + half, hs=(h,))

    def finish(job, h, half, more_parts=(), more_stats=()):
        b = b_own[h]
        await_results(job, *((3, 4), (2, 5))[half], hs=(h,))
        parts = [part_buf.at[job, h, b], in_buf.at[job, h, 1], in_buf.at[job, h, 2], *more_parts]
        stats = [lse_buf[job, h, b, half], in_lse[job, h, 1, half], in_lse[job, h, 2, half], *more_stats]
        scales, whole = weights(stats)
        return [merge(parts, scales, g) for g in (2 * half, 2 * half + 1)], whole

    def order(i):
        return jnp.where(i == 0, 2, jnp.where(i == 1, 1, jnp.where(i == 2, 3, 0)))

    def local_step(i, carry):
        for h in range(2):
            local_shard(h, order(i))
        @pl.when(i == 0)
        def _():
            send_results(0, 0, 1)
            on(mem_b_rings, WAIT, 0, 1)
            on(mem_b_rings, SEND, 4, 5)

        pl.when(i == 1)(lambda: send_results(0, 2))
        pl.when(i == 2)(lambda: send_results(0, 3))
        return carry

    lax.fori_loop(0, SIDE, local_step, 0)

    for h in range(2):
        for d in range(SIDE):
            for dz in range(2):
                if d or dz:
                    tab_in(h, d, dz).wait_recv()
    to_smem = pltpu.make_async_copy(tab_buf, tab_sm, l_sem.at[count])
    to_smem.start()
    to_smem.wait()
    pass_on(0)
    on(mem_a_rings, WAIT, 2, 3, 4, 5)
    on(mem_b_rings, WAIT, 2, 3, 4, 5)
    for h in range(2):
        for d in range(SIDE):
            q_z_in(h, d).wait_recv()

    lane = lax.broadcasted_iota(jnp.int32, (1, 2 * MBLK), 1)

    def memory_shard(job, h, b, pz):
        for blk in range(2):
            tok = slice(blk * QBLK, (blk + 1) * QBLK)
            keys, vals, bias = [], [], []
            for a in range(SIDE):
                shard = (a * 4 + y) * 2 + z if h == 0 else (x * 4 + a) * 2 + z
                slots = [tab_sm[h, b, pz, 2 * blk + k, shard] for k in range(2)]
                for slot in slots:
                    at = jnp.clip(slot, 0, SHARD_BLOCKS - 1)
                    keys.append(mem_buf[h, a, 0, at])
                    vals.append(mem_buf[h, a, 1, at])
                off = [jnp.where(slot < 0, NEG, 0.0) for slot in slots]
                bias.append(jnp.where(lane < MBLK, off[0], off[1]))
            keys = jnp.concatenate(keys, axis=0)
            vals = with_ones(jnp.concatenate(vals, axis=0))
            bias = jnp.concatenate(bias, axis=1)
            sums = []
            for g in range(SHARE):
                s = dot_nt(q_buf[h, b, pz, g, tok, :], keys) + bias
                top = jnp.max(s, axis=1, keepdims=True)
                p = jnp.exp2((s - top) * FACTOR).astype(jnp.bfloat16)
                both = jnp.dot(p, vals, preferred_element_type=jnp.float32)
                total = both[:, DH:]
                part_buf[job, h, b, g, tok, :] = (both[:, :DH] / total).astype(jnp.bfloat16)
                sums.append(top * FACTOR + jnp.log2(total))
            lse_buf[job, h, b, 0, :, tok] = rows_of(sums[:2])
            lse_buf[job, h, b, 1, :, tok] = rows_of(sums[2:])

    def z_copies(h, half):
        heads = pl.ds(2 * half, 2)
        n = 2 * h + half
        return (
            remote(z_part.at[h, heads], z_in.at[h, heads], z_s.at[n], z_r.at[n], z_peer),
            remote(z_lse.at[h, half], z_lse_in.at[h, half], zs_s.at[n], zs_r.at[n], z_peer),
        )

    def to_z_peer():
        for half in range(2):
            for h in range(2):
                results, whole = finish(1, h, half)
                for k in range(2):
                    z_part[h, 2 * half + k] = results[k].astype(jnp.bfloat16)
                z_lse[h, half] = whole
                for cp in z_copies(h, half):
                    cp.start()

    def memory_step(i, carry):
        job = 1 + i // SIDE
        for h in range(2):
            memory_shard(job, h, wrap(b_own[h] + order(i % SIDE)), jnp.where(job == 1, zo, z))
        pl.when(i == 0)(lambda: send_results(1, 0, 1))
        pl.when(i == 1)(lambda: send_results(1, 2))
        pl.when(i == 2)(lambda: send_results(1, 3))
        pl.when(i == 3)(lambda: pass_on(1))
        pl.when(i == 4)(lambda: send_results(2, 0, 1))
        pl.when(i == 5)(lambda: send_results(2, 2))
        pl.when(i == 5)(to_z_peer)
        pl.when(i == 6)(lambda: send_results(2, 3))
        pl.when(i == 7)(lambda: pass_on(2))
        return carry

    lax.fori_loop(0, 2 * SIDE, memory_step, 0)

    def gate_dot(which, fin, head):
        feats = slice(head * DH, (head + 1) * DH)
        return dot_nt(gw_ref[which, :, feats], fin[head].astype(jnp.bfloat16))

    logits = jnp.zeros((GROUPS * HEADS_DEV, ROWS), jnp.float32)
    for half in range(2):
        for h in range(2):
            results, _ = finish(0, h, half)
            for k in range(2):
                head = h * SHARE + 2 * half + k
                loc_fin[head] = results[k]
                logits += gate_dot(0, loc_fin, head)
    for half in range(2):
        for h in range(2):
            for cp in z_copies(h, half):
                cp.wait_recv()
            results, _ = finish(2, h, half, [z_in.at[h]], [z_lse_in[h, half]])
            for k in range(2):
                head = h * SHARE + 2 * half + k
                mem_fin[head] = results[k]
                logits += gate_dot(1, mem_fin, head)
    lg_out[...] = logits.reshape(GROUPS, HEADS_DEV, ROWS)

    def lg(d):
        to = lax.rem(g_own + d, GROUPS)
        return remote(lg_out.at[to], lg_in.at[d], lg_s.at[d], lg_r.at[d], (c, to))

    for d in range(1, GROUPS):
        go(lg(d))
    own = lg_out[g_own]
    for d in range(1, GROUPS):
        lg(d).wait_recv()
        own = own + lg_in[d]
    gate = jax.nn.sigmoid(jnp.transpose(own) + gb_ref[...])
    for head in range(HEADS_DEV):
        share = gate[:, head : head + 1]
        mixed = share * mem_fin[head] + (1.0 - share) * loc_fin[head]
        out_ref[:, head * DH : (head + 1) * DH] = mixed.astype(jnp.bfloat16)

    for h in range(2):
        for job in range(3):
            for n in range(6):
                for cp in result_copies(job, h, n):
                    cp.wait_send()
        for half in range(2):
            for cp in z_copies(h, half):
                cp.wait_send()
    for rings in (q_rings, kv_rings, kvo_rings, mem_a_rings, mem_b_rings):
        on(rings, SENT, *range(6))
    for cp in started:
        cp.wait_send()


def on_device(queries, keys, values, mem_keys, mem_values, retrieval, gate_weight, gate_bias):
    bf, f32 = jnp.bfloat16, jnp.float32
    dma = pltpu.SemaphoreType.DMA
    anywhere = pl.BlockSpec(memory_space=pl.ANY)
    vmem = pl.BlockSpec(memory_space=pltpu.VMEM)
    part = (SHARE, ROWS, DH)
    stat = (8, ROWS)
    return pl.pallas_call(
        kernel,
        out_shape=jax.ShapeDtypeStruct((ROWS, HEADS_DEV * DH), bf),
        in_specs=[anywhere] * 5 + [vmem] * 3,
        out_specs=vmem,
        scratch_shapes=[
            pltpu.VMEM((2, SIDE, 2) + part, bf),
            pltpu.VMEM((2, SIDE, 2, 2, ROWS, DH), bf),
            pltpu.VMEM((2, SIDE, 2, SHARD_BLOCKS, MBLK, DH), bf),
            pltpu.VMEM((2, SIDE, 2, 8, 128), jnp.int32),
            pltpu.SMEM((2, SIDE, 2, 8, 128), jnp.int32),
            pltpu.VMEM((3, 2, SIDE) + part, bf),
            pltpu.VMEM((3, 2, SIDE, 2) + stat, f32),
            pltpu.VMEM((3, 2, 3) + part, bf),
            pltpu.VMEM((3, 2, 3, 2) + stat, f32),
            pltpu.VMEM((2,) + part, bf),
            pltpu.VMEM((2, 2) + stat, f32),
            pltpu.VMEM((2,) + part, bf),
            pltpu.VMEM((2, 2) + stat, f32),
            pltpu.VMEM((HEADS_DEV, ROWS, DH), f32),
            pltpu.VMEM((HEADS_DEV, ROWS, DH), f32),
            pltpu.VMEM((2 * SHARE, QBLK, 2 * DH), f32),
            pltpu.VMEM((2 * SHARE, QBLK, DH), f32),
            pltpu.VMEM((GROUPS, HEADS_DEV, ROWS), f32),
            pltpu.VMEM((GROUPS, HEADS_DEV, ROWS), f32),
            dma((24,)),
            dma((2,)), dma((2,)),
            dma((2, 2, 6)), dma((2, 2, 6)),
            dma((2, 6)), dma((2, 6)),
            dma((2, SIDE)), dma((2, SIDE)),
            dma((2, 8)), dma((2, 8)),
            dma((2, 2, 6)), dma((2, 2, 6)),
            dma((3, 2, 6)), dma((3, 2, 6)),
            dma((3, 2, 6)), dma((3, 2, 6)),
            dma((4,)), dma((4,)),
            dma((4,)), dma((4,)),
            dma((SIDE,)), dma((SIDE,)),
        ],
        compiler_params=pltpu.CompilerParams(
            collective_id=0, has_side_effects=True, vmem_limit_bytes=60 * 2**20
        ),
    )(
        queries, keys, values, mem_keys, mem_values, retrieval.reshape(2, -1),
        gate_weight.transpose(0, 2, 1), gate_bias.reshape(1, HEADS_DEV),
    )


def solution(mesh):
    placed = (
        P("ctx", "mem"),
        P("ctx", "mem"),
        P("ctx", "mem"),
        P("ctx", None, "mem"),
        P("ctx", None, "mem"),
        P("ctx", "mem", None),
        P(None, "mem", None),
        P("mem"),
    )
    return jax.shard_map(
        on_device, mesh=mesh, in_specs=placed, out_specs=P("ctx", "mem"), check_vma=False
    )
```

```python
import functools
import math

import jax
import jax.numpy as jnp
from jax import lax
from jax.experimental import pallas as pl
from jax.experimental.pallas import tpu as pltpu
from jax.sharding import PartitionSpec as P

MESH = pl.DeviceIdType.MESH
SIDE = 4
DH = 128
SHARE = 4
QBLK = 128
ROWS = 256
SHARD_BLOCKS = 32
MBLK = 64
GROUPS = 4
HEADS_DEV = 8
NEG = -1e30
FACTOR = DH**-0.5 * math.log2(math.e)


def dot_nt(a, b):
    return lax.dot_general(a, b, (((1,), (1,)), ((), ())), preferred_element_type=jnp.float32)


def with_ones(v):
    return jnp.concatenate([v, jnp.ones_like(v)], axis=1)


def rows_of(pieces):
    shape = (QBLK, QBLK)
    eye = lax.broadcasted_iota(jnp.int32, shape, 0) == lax.broadcasted_iota(jnp.int32, shape, 1)
    rows = [jnp.sum(jnp.where(eye, piece, 0.0), axis=0, keepdims=True) for piece in pieces]
    return jnp.concatenate(rows + [jnp.zeros((6, QBLK), jnp.float32)], axis=0)


def block_table(ids):
    shape = (SHARD_BLOCKS, SHARD_BLOCKS)
    shard = lax.broadcasted_iota(jnp.int32, shape, 0)
    lane = lax.broadcasted_iota(jnp.int32, (SHARD_BLOCKS, 128), 1)
    table = jnp.full((SHARD_BLOCKS, 128), -1, jnp.int32)
    for l in range(2):
        row = ids[l : l + 1, :]
        held = row // SHARD_BLOCKS == shard
        offset = row % SHARD_BLOCKS + jnp.zeros_like(shard)
        low = jnp.min(jnp.where(held, offset, 99), axis=1, keepdims=True)
        high = jnp.max(jnp.where(held, offset, -1), axis=1, keepdims=True)
        first = jnp.where(low > 90, -1, low)
        second = jnp.where(high > low, high, -1)
        table = jnp.where(lane == 2 * l, first, jnp.where(lane == 2 * l + 1, second, table))
    turned = jnp.transpose(table)[:8]
    return jnp.concatenate([turned, jnp.full((8, 96), -1, jnp.int32)], axis=1)


def kernel(
    q_hbm, k_hbm, v_hbm, mk_hbm, mv_hbm, ids_hbm, gw_hbm, gb_hbm,
    out_ref,
    q_buf, kv_buf, mem_buf, tab_buf, tab_sm,
    part_buf, lse_buf, in_buf, in_lse, z_part, z_lse, z_in, z_lse_in,
    loc_fin, mem_fin, acc_ref, max_ref, lg_out, lg_in, ids_ref, gw_ref, gb_ref,
    l_sem, kvz_s, kvz_r, kva_s, kva_r, qb_s, qb_r, qz_s, qz_r, tab_s, tab_r, ma_s, ma_r,
    rs_s, rs_r, rl_s, rl_r, z_s, z_r, zs_s, zs_r, lg_s, lg_r,
):
    c = lax.axis_index("ctx")
    g_own = lax.axis_index("mem")
    x, y, z = c // 8, (c // 2) % 4, c % 2
    zo = 1 - z

    def wrap(i):
        return lax.rem(i + SIDE, SIDE)

    def device(px, py, pz):
        return (px * 8 + py * 2 + pz, g_own)

    def key_peer(h, d):
        return device(wrap(x + d), y, z) if h == 0 else device(x, wrap(y + d), z)

    def query_peer(h, d):
        if isinstance(h, int):
            return key_peer(1 - h, d)
        px = jnp.where(h == 0, x, wrap(x + d))
        return device(px, jnp.where(h == 0, wrap(y + d), y), z)

    def query_own(h):
        return b_own[h] if isinstance(h, int) else jnp.where(h == 0, y, x)

    z_peer = device(x, y, zo)
    a_own = (x, y)
    b_own = (y, x)

    def remote(src, dst, ssem, rsem, peer):
        return pltpu.make_async_remote_copy(
            src_ref=src, dst_ref=dst, send_sem=ssem, recv_sem=rsem,
            device_id=peer, device_id_type=MESH,
        )

    kv_local, q_local, mem_local, small_local = [], [], [], []
    count = 0

    def local(src, dst, group):
        nonlocal count
        cp = pltpu.make_async_copy(src, dst, l_sem.at[count])
        cp.start()
        group.append(cp)
        count += 1

    for h in range(2):
        cols = pl.ds(h * DH, DH)
        local(k_hbm.at[:, cols], kv_buf.at[h, a_own[h], 0, z], kv_local)
        local(v_hbm.at[:, cols], kv_buf.at[h, a_own[h], 1, z], kv_local)
    for h in range(2):
        for g in range(SHARE):
            local(
                q_hbm.at[:, pl.ds((h * SHARE + g) * DH, DH)],
                q_buf.at[h, b_own[h], z, g],
                q_local,
            )
    for h in range(2):
        cols = pl.ds(h * DH, DH)
        local(mk_hbm.at[:, :, cols], mem_buf.at[h, a_own[h], 0], mem_local)
        local(mv_hbm.at[:, :, cols], mem_buf.at[h, a_own[h], 1], mem_local)

    local(ids_hbm, ids_ref, small_local)
    local(gw_hbm, gw_ref, small_local)
    local(gb_hbm, gb_ref, small_local)

    barrier = pltpu.get_barrier_semaphore()
    greeted = [z_peer]
    for d in (1, 3):
        greeted += [device(wrap(x + d), y, z), device(x, wrap(y + d), z)]
    for d in range(1, GROUPS):
        greeted += [(c, lax.rem(g_own + d, GROUPS))]
    for peer in greeted:
        pl.semaphore_signal(barrier, inc=1, device_id=peer, device_id_type=MESH)
    pl.semaphore_wait(barrier, len(greeted))

    started = []

    def go(cp):
        cp.start()
        started.append(cp)
        return cp

    def kv_z(h):
        ref = kv_buf.at[h, a_own[h], :, z]
        return remote(ref, ref, kvz_s.at[h], kvz_r.at[h], z_peer)

    def kv_z_in(h):
        ref = kv_buf.at[h, a_own[h], :, zo]
        return remote(ref, ref, kvz_s.at[h], kvz_r.at[h], z_peer)

    def ring(h, own, peer, ref, ssem, rsem):
        left, right, across = wrap(own - 1), wrap(own + 1), wrap(own + 2)
        out = [(own, 0, 1), (own, 1, 3), (own, 1, 1), (own, 0, 3), (left, 0, 1), (right, 1, 3)]
        come = [(left, 0), (right, 1), (left, 1), (right, 0), (across, 0), (across, 1)]

        def copy(n):
            at, half, d = out[n]
            return remote(ref(at, half), ref(at, half), ssem.at[n], rsem.at[n], peer(h, d))

        def send(n):
            copy(n).start()

        def sent(n):
            copy(n).wait_send()

        def wait(n):
            at, half = come[n]
            remote(ref(at, half), ref(at, half), ssem.at[n], rsem.at[n], z_peer).wait_recv()

        return send, wait, sent

    def kv_ring(h, part):
        pz = (z, zo)[part]
        return ring(
            h, a_own[h], key_peer, lambda at, half: kv_buf.at[h, at, half, pz],
            kva_s.at[h, part], kva_r.at[h, part],
        )

    def q_ring(h):
        return ring(
            h, b_own[h], query_peer, lambda at, half: q_buf.at[h, at, z, pl.ds(2 * half, 2)],
            qb_s.at[h], qb_r.at[h],
        )

    def mem_ring(h, part):
        blocks = pl.ds(part * (SHARD_BLOCKS // 2), SHARD_BLOCKS // 2)
        return ring(
            h, a_own[h], key_peer, lambda at, half: mem_buf.at[h, at, half, blocks],
            ma_s.at[h, part], ma_r.at[h, part],
        )

    def q_z(h, d):
        ref = q_buf.at[h, wrap(b_own[h] + d), z]
        return remote(ref, ref, qz_s.at[h, d], qz_r.at[h, d], z_peer)

    def q_z_in(h, d):
        ref = q_buf.at[h, wrap(b_own[h] + d), zo]
        return remote(ref, ref, qz_s.at[h, d], qz_r.at[h, d], z_peer)

    def tab(h, n, at, pz, peer):
        ref = tab_buf.at[h, wrap(b_own[h] + at), pz]
        return remote(ref, ref, tab_s.at[h, n], tab_r.at[h, n], peer)

    def tab_out(h, n):
        at, way = ((0, 1), (0, 3), (-1, 1))[n]
        return tab(h, n, at, z, query_peer(h, way))

    def tab_in(h, n):
        return tab(h, n, (-1, 1, 2)[n], z, z_peer)

    def tab_z(h, d, pz):
        return tab(h, 3 + d, d, pz, z_peer)

    q_rings = [q_ring(h) for h in range(2)]
    kv_rings = [kv_ring(h, 0) for h in range(2)]
    kvo_rings = [kv_ring(h, 1) for h in range(2)]
    mem_a_rings = [mem_ring(h, 0) for h in range(2)]
    mem_b_rings = [mem_ring(h, 1) for h in range(2)]

    def on(rings, what, *steps):
        for n in steps:
            for r in rings:
                r[what](n)

    SEND, WAIT, SENT = 0, 1, 2
    for cp in kv_local:
        cp.wait()
    for h in range(2):
        go(kv_z(h))
    for cp in q_local:
        cp.wait()
    on(q_rings, SEND, 0, 1)
    on(kv_rings, SEND, 0, 1)
    on(q_rings, SEND, 2, 3)
    on(kv_rings, SEND, 2, 3)
    for h in range(2):
        go(q_z(h, 0))
    for cp in mem_local:
        cp.wait()
    on(mem_a_rings, SEND, 0, 1)
    for cp in small_local:
        cp.wait()
    for h in range(2):
        tab_buf[h, b_own[h], z] = block_table(ids_ref[...])
    for h in range(2):
        go(tab_out(h, 0))
        go(tab_out(h, 1))
        go(tab_z(h, 0, z))
    for h in range(2):
        kv_z_in(h).wait_recv()
    on(kvo_rings, SEND, 0, 1, 2, 3)
    on(q_rings, WAIT, 0, 1)
    on(q_rings, SEND, 4, 5)
    on(kv_rings, WAIT, 0, 1)
    on(kv_rings, SEND, 4, 5)
    on(mem_a_rings, SEND, 2, 3)
    on(q_rings, WAIT, 2, 3)
    for h in range(2):
        go(q_z(h, 1))
        go(q_z(h, 3))
    on(kvo_rings, WAIT, 0, 1)
    on(kvo_rings, SEND, 4, 5)
    for h in range(2):
        tab_in(h, 0).wait_recv()
        tab_in(h, 1).wait_recv()
        go(tab_out(h, 2))
        go(tab_z(h, 3, z))
        go(tab_z(h, 1, z))
    on(mem_b_rings, SEND, 0, 1, 2, 3)
    on(q_rings, WAIT, 4, 5)
    for h in range(2):
        go(q_z(h, 2))
    on(kv_rings, WAIT, 2, 3, 4, 5)
    on(kvo_rings, WAIT, 2, 3, 4, 5)
    for h in range(2):
        tab_in(h, 2).wait_recv()
        go(tab_z(h, 2, z))
    on(mem_a_rings, WAIT, 0, 1)
    on(mem_a_rings, SEND, 4, 5)

    def local_shard(h, d):
        b = wrap(b_own[h] + d)
        if h == 0:
            tiles = x + jnp.where(y <= b, 1, 0)
            q_shard = (x * 4 + b) * 2 + z
        else:
            tiles = jnp.where(x < b, 4, jnp.where(x == b, y + 1, 0))
            q_shard = (b * 4 + y) * 2 + z
        lane_blk = lax.broadcasted_iota(jnp.int32, (1, 512), 1) // QBLK

        acc_ref[...] = jnp.zeros_like(acc_ref)
        max_ref[...] = jnp.full_like(max_ref, NEG)

        def tile(a, carry):
            k_shard = (a * 4 + y) * 2 if h == 0 else (x * 4 + a) * 2
            keys = kv_buf[h, a, 0].reshape(512, DH)
            vals = with_ones(kv_buf[h, a, 1].reshape(512, DH))
            for blk in range(2):
                seen = k_shard * 2 + lane_blk <= q_shard * 2 + blk
                bias = jnp.where(seen, 0.0, NEG)
                for g in range(SHARE):
                    n = blk * SHARE + g
                    q = q_buf[h, b, z, g, blk * QBLK : (blk + 1) * QBLK, :]
                    s = dot_nt(q, keys) + bias
                    old = max_ref[n]
                    new = jnp.maximum(old, jnp.max(s, axis=1, keepdims=True))
                    wide = jnp.concatenate([new] * 4, axis=1)
                    p = jnp.exp2((s - wide) * FACTOR).astype(jnp.bfloat16)
                    fade = jnp.exp2((old - new) * FACTOR)
                    add = jnp.dot(p, vals, preferred_element_type=jnp.float32)
                    acc_ref[n, :, :DH] = acc_ref[n, :, :DH] * fade + add[:, :DH]
                    acc_ref[n, :, DH:] = acc_ref[n, :, DH:] * fade + add[:, DH:]
                    max_ref[n] = new
            return carry

        lax.fori_loop(0, tiles, tile, 0)
        for blk in range(2):
            tok = slice(blk * QBLK, (blk + 1) * QBLK)
            sums = []
            for g in range(SHARE):
                n = blk * SHARE + g
                total = acc_ref[n, :, DH:]
                some = total > 0.0
                safe = jnp.where(some, total, 1.0)
                part_buf[0, h, b, g, tok, :] = (acc_ref[n, :, :DH] / safe).astype(jnp.bfloat16)
                sums.append(jnp.where(some, max_ref[n] * FACTOR + jnp.log2(safe), NEG))
            lse_buf[0, h, b, 0, :, tok] = rows_of(sums[:2])
            lse_buf[0, h, b, 1, :, tok] = rows_of(sums[2:])

    MESSAGES = [(2, 0, 1, 0), (2, 1, 3, 0), (1, 1, 1, 1), (3, 0, 3, 2), (1, 0, 1, 1), (3, 1, 3, 2)]

    def result_copies(job, h, n, whose, half, way, lands):
        b = wrap(query_own(h) + whose)
        heads = pl.ds(2 * half, 2)
        peer = query_peer(h, way)
        return (
            remote(
                part_buf.at[job, h, b, heads], in_buf.at[job, h, lands, heads],
                rs_s.at[job, h, n], rs_r.at[job, h, n], peer,
            ),
            remote(
                lse_buf.at[job, h, b, half], in_lse.at[job, h, lands, half],
                rl_s.at[job, h, n], rl_r.at[job, h, n], peer,
            ),
        )

    def send_results(job, *numbers):
        for n in numbers:
            for h in range(2):
                for cp in result_copies(job, h, n, *MESSAGES[n]):
                    cp.start()

    def each_pair(body, init=0):
        for m in range(4):
            init = body(m % 2, m // 2, init)
        return init

    def weights(stats):
        top = functools.reduce(jnp.maximum, stats)
        powers = [jnp.exp2(s - top) for s in stats]
        total = functools.reduce(jnp.add, powers)
        scales = [jnp.transpose(p / total) for p in powers]
        return scales, top + jnp.log2(total)

    def merge(parts, scales, half, k):
        total = None
        for part, scale in zip(parts, scales):
            term = part[2 * half + k].astype(jnp.float32) * scale[:, k : k + 1]
            total = term if total is None else total + term
        return total

    def pass_on(job):
        def pair(h, half, carry):
            way = 1 + 2 * half
            for cp in result_copies(job, h, half, 2, half, way, 0):
                cp.wait_recv()
            b = wrap(query_own(h) + way)
            mine, other = part_buf.at[job, h, b], in_buf.at[job, h, 0]
            scales, whole = weights([lse_buf[job, h, b, half], in_lse[job, h, 0, half]])
            for k in range(2):
                mine[2 * half + k] = merge([mine, other], scales, half, k).astype(jnp.bfloat16)
            lse_buf[job, h, b, half] = whole
            for cp in result_copies(job, h, 4 + half, way, half, way, 1 + half):
                cp.start()
            return carry

        each_pair(pair)

    def finish(job, h, half, more_parts=(), more_stats=()):
        b = query_own(h)
        left, right = jnp.where(half == 0, 4, 2), jnp.where(half == 0, 3, 5)
        for n, lands in ((left, 1), (right, 2)):
            for cp in result_copies(job, h, n, 0, half, 1, lands):
                cp.wait_recv()
        parts = [part_buf.at[job, h, b], in_buf.at[job, h, 1], in_buf.at[job, h, 2], *more_parts]
        stats = [lse_buf[job, h, b, half], in_lse[job, h, 1, half], in_lse[job, h, 2, half], *more_stats]
        scales, whole = weights(stats)
        return [merge(parts, scales, half, k) for k in range(2)], whole

    def order(i):
        return jnp.where(i == 0, 2, jnp.where(i == 1, 1, jnp.where(i == 2, 3, 0)))

    def local_step(i, carry):
        for h in range(2):
            local_shard(h, order(i))
        @pl.when(i == 0)
        def _():
            send_results(0, 0, 1)
            on(mem_b_rings, WAIT, 0, 1)
            on(mem_b_rings, SEND, 4, 5)

        pl.when(i == 1)(lambda: send_results(0, 2))
        pl.when(i == 2)(lambda: send_results(0, 3))
        return carry

    lax.fori_loop(0, SIDE, local_step, 0)

    for h in range(2):
        for d in range(SIDE):
            tab_z(h, d, zo).wait_recv()
    to_smem = pltpu.make_async_copy(tab_buf, tab_sm, l_sem.at[count])
    to_smem.start()
    to_smem.wait()
    on(mem_a_rings, WAIT, 2, 3, 4, 5)
    on(mem_b_rings, WAIT, 2, 3, 4, 5)
    for h in range(2):
        for d in range(SIDE):
            q_z_in(h, d).wait_recv()

    lane = lax.broadcasted_iota(jnp.int32, (1, 2 * MBLK), 1)

    def memory_shard(job, h, b, pz):
        for blk in range(2):
            tok = slice(blk * QBLK, (blk + 1) * QBLK)
            keys, vals, bias = [], [], []
            for a in range(SIDE):
                shard = (a * 4 + y) * 2 + z if h == 0 else (x * 4 + a) * 2 + z
                slots = [tab_sm[h, b, pz, 2 * blk + k, shard] for k in range(2)]
                for slot in slots:
                    at = jnp.clip(slot, 0, SHARD_BLOCKS - 1)
                    keys.append(mem_buf[h, a, 0, at])
                    vals.append(mem_buf[h, a, 1, at])
                off = [jnp.where(slot < 0, NEG, 0.0) for slot in slots]
                bias.append(jnp.where(lane < MBLK, off[0], off[1]))
            keys = jnp.concatenate(keys, axis=0)
            vals = with_ones(jnp.concatenate(vals, axis=0))
            bias = jnp.concatenate(bias, axis=1)
            sums = []
            for g in range(SHARE):
                s = dot_nt(q_buf[h, b, pz, g, tok, :], keys) + bias
                top = jnp.max(s, axis=1, keepdims=True)
                p = jnp.exp2((s - top) * FACTOR).astype(jnp.bfloat16)
                both = jnp.dot(p, vals, preferred_element_type=jnp.float32)
                total = both[:, DH:]
                part_buf[job, h, b, g, tok, :] = (both[:, :DH] / total).astype(jnp.bfloat16)
                sums.append(top * FACTOR + jnp.log2(total))
            lse_buf[job, h, b, 0, :, tok] = rows_of(sums[:2])
            lse_buf[job, h, b, 1, :, tok] = rows_of(sums[2:])

    def z_copies(h, half):
        heads = pl.ds(2 * half, 2)
        n = 2 * h + half
        return (
            remote(z_part.at[h, heads], z_in.at[h, heads], z_s.at[n], z_r.at[n], z_peer),
            remote(z_lse.at[h, half], z_lse_in.at[h, half], zs_s.at[n], zs_r.at[n], z_peer),
        )

    def to_z_peer():
        def pair(h, half, carry):
            results, whole = finish(1, h, half)
            for k in range(2):
                z_part[h, 2 * half + k] = results[k].astype(jnp.bfloat16)
            z_lse[h, half] = whole
            for cp in z_copies(h, half):
                cp.start()
            return carry

        each_pair(pair)

    def memory_step(i, carry):
        job = 1 + i // SIDE
        for h in range(2):
            memory_shard(job, h, wrap(b_own[h] + order(i % SIDE)), jnp.where(job == 1, zo, z))
        pl.when(i == 0)(lambda: send_results(1, 0, 1))
        pl.when(i == 1)(lambda: send_results(1, 2))
        pl.when(i == 2)(lambda: send_results(1, 3))
        pl.when(i == 3)(lambda: pass_on(1))
        pl.when(i == 4)(lambda: send_results(2, 0, 1))
        pl.when(i == 4)(lambda: pass_on(0))
        pl.when(i == 5)(lambda: send_results(2, 2))
        pl.when(i == 5)(to_z_peer)
        pl.when(i == 6)(lambda: send_results(2, 3))
        pl.when(i == 7)(lambda: pass_on(2))
        return carry

    lax.fori_loop(0, 2 * SIDE, memory_step, 0)

    def gate_dot(which, fin, head):
        feats = pl.ds(pl.multiple_of(head * DH, DH), DH)
        return dot_nt(gw_ref[which, :, feats], fin[head].astype(jnp.bfloat16))

    def local_pair(h, half, logits):
        results, _ = finish(0, h, half)
        for k in range(2):
            head = h * SHARE + 2 * half + k
            loc_fin[head] = results[k]
            logits += gate_dot(0, loc_fin, head)
        return logits

    def memory_pair(h, half, logits):
        for cp in z_copies(h, half):
            cp.wait_recv()
        results, _ = finish(2, h, half, [z_in.at[h]], [z_lse_in[h, half]])
        for k in range(2):
            head = h * SHARE + 2 * half + k
            mem_fin[head] = results[k]
            logits += gate_dot(1, mem_fin, head)
        return logits

    logits = each_pair(local_pair, jnp.zeros((GROUPS * HEADS_DEV, ROWS), jnp.float32))
    logits = each_pair(memory_pair, logits)
    lg_out[...] = logits.reshape(GROUPS, HEADS_DEV, ROWS)

    def lg(d):
        to = lax.rem(g_own + d, GROUPS)
        return remote(lg_out.at[to], lg_in.at[d], lg_s.at[d], lg_r.at[d], (c, to))

    for d in range(1, GROUPS):
        go(lg(d))
    own = lg_out[g_own]
    for d in range(1, GROUPS):
        lg(d).wait_recv()
        own = own + lg_in[d]
    gate = jax.nn.sigmoid(jnp.transpose(own) + gb_ref[...])
    for head in range(HEADS_DEV):
        share = gate[:, head : head + 1]
        mixed = share * mem_fin[head] + (1.0 - share) * loc_fin[head]
        out_ref[:, head * DH : (head + 1) * DH] = mixed.astype(jnp.bfloat16)

    for h in range(2):
        for job in range(3):
            for n in range(6):
                for cp in result_copies(job, h, n, *MESSAGES[n]):
                    cp.wait_send()
        for half in range(2):
            for cp in z_copies(h, half):
                cp.wait_send()
    for rings in (q_rings, kv_rings, kvo_rings, mem_a_rings, mem_b_rings):
        on(rings, SENT, *range(6))
    for cp in started:
        cp.wait_send()


def on_device(queries, keys, values, mem_keys, mem_values, retrieval, gate_weight, gate_bias):
    bf, f32 = jnp.bfloat16, jnp.float32
    dma = pltpu.SemaphoreType.DMA
    hbm = pl.BlockSpec(memory_space=pltpu.HBM)
    vmem = pl.BlockSpec(memory_space=pltpu.VMEM)
    part = (SHARE, ROWS, DH)
    stat = (8, ROWS)
    return pl.pallas_call(
        kernel,
        out_shape=jax.ShapeDtypeStruct((ROWS, HEADS_DEV * DH), bf),
        in_specs=[hbm] * 8,
        out_specs=vmem,
        scratch_shapes=[
            pltpu.VMEM((2, SIDE, 2) + part, bf),
            pltpu.VMEM((2, SIDE, 2, 2, ROWS, DH), bf),
            pltpu.VMEM((2, SIDE, 2, SHARD_BLOCKS, MBLK, DH), bf),
            pltpu.VMEM((2, SIDE, 2, 8, 128), jnp.int32),
            pltpu.SMEM((2, SIDE, 2, 8, 128), jnp.int32),
            pltpu.VMEM((3, 2, SIDE) + part, bf),
            pltpu.VMEM((3, 2, SIDE, 2) + stat, f32),
            pltpu.VMEM((3, 2, 3) + part, bf),
            pltpu.VMEM((3, 2, 3, 2) + stat, f32),
            pltpu.VMEM((2,) + part, bf),
            pltpu.VMEM((2, 2) + stat, f32),
            pltpu.VMEM((2,) + part, bf),
            pltpu.VMEM((2, 2) + stat, f32),
            pltpu.VMEM((HEADS_DEV, ROWS, DH), f32),
            pltpu.VMEM((HEADS_DEV, ROWS, DH), f32),
            pltpu.VMEM((2 * SHARE, QBLK, 2 * DH), f32),
            pltpu.VMEM((2 * SHARE, QBLK, DH), f32),
            pltpu.VMEM((GROUPS, HEADS_DEV, ROWS), f32),
            pltpu.VMEM((GROUPS, HEADS_DEV, ROWS), f32),
            pltpu.VMEM((2, 32), jnp.int32),
            pltpu.VMEM((2, GROUPS * HEADS_DEV, HEADS_DEV * DH), bf),
            pltpu.VMEM((1, HEADS_DEV), f32),
            dma((24,)),
            dma((2,)), dma((2,)),
            dma((2, 2, 6)), dma((2, 2, 6)),
            dma((2, 6)), dma((2, 6)),
            dma((2, SIDE)), dma((2, SIDE)),
            dma((2, 8)), dma((2, 8)),
            dma((2, 2, 6)), dma((2, 2, 6)),
            dma((3, 2, 6)), dma((3, 2, 6)),
            dma((3, 2, 6)), dma((3, 2, 6)),
            dma((4,)), dma((4,)),
            dma((4,)), dma((4,)),
            dma((SIDE,)), dma((SIDE,)),
        ],
        compiler_params=pltpu.CompilerParams(
            collective_id=0, has_side_effects=True, vmem_limit_bytes=60 * 2**20
        ),
    )(
        queries, keys, values, mem_keys, mem_values, retrieval.reshape(2, -1),
        gate_weight.transpose(0, 2, 1), gate_bias.reshape(1, HEADS_DEV),
    )


def solution(mesh):
    placed = (
        P("ctx", "mem"),
        P("ctx", "mem"),
        P("ctx", "mem"),
        P("ctx", None, "mem"),
        P("ctx", None, "mem"),
        P("ctx", "mem", None),
        P(None, "mem", None),
        P("mem"),
    )
    return jax.shard_map(
        on_device, mesh=mesh, in_specs=placed, out_specs=P("ctx", "mem"), check_vma=False
    )
```

```python
import functools
import math

import jax
import jax.numpy as jnp
from jax import lax
from jax.experimental import pallas as pl
from jax.experimental.pallas import tpu as pltpu
from jax.sharding import PartitionSpec as P

MESH = pl.DeviceIdType.MESH
SIDE = 4
DH = 128
SHARE = 4
QBLK = 128
ROWS = 256
SHARD_BLOCKS = 32
MBLK = 64
GROUPS = 4
HEADS_DEV = 8
NEG = -1e30
FACTOR = DH**-0.5 * math.log2(math.e)


def dot_nt(a, b):
    return lax.dot_general(a, b, (((1,), (1,)), ((), ())), preferred_element_type=jnp.float32)


def with_ones(v):
    return jnp.concatenate([v, jnp.ones_like(v)], axis=1)


def rows_of(pieces):
    shape = (QBLK, QBLK)
    eye = lax.broadcasted_iota(jnp.int32, shape, 0) == lax.broadcasted_iota(jnp.int32, shape, 1)
    rows = [jnp.sum(jnp.where(eye, piece, 0.0), axis=0, keepdims=True) for piece in pieces]
    return jnp.concatenate(rows + [jnp.zeros((6, QBLK), jnp.float32)], axis=0)


def block_table(ids):
    shape = (SHARD_BLOCKS, SHARD_BLOCKS)
    shard = lax.broadcasted_iota(jnp.int32, shape, 0)
    lane = lax.broadcasted_iota(jnp.int32, (SHARD_BLOCKS, 128), 1)
    table = jnp.full((SHARD_BLOCKS, 128), -1, jnp.int32)
    for l in range(2):
        row = ids[l : l + 1, :]
        held = row // SHARD_BLOCKS == shard
        offset = row % SHARD_BLOCKS + jnp.zeros_like(shard)
        low = jnp.min(jnp.where(held, offset, 99), axis=1, keepdims=True)
        high = jnp.max(jnp.where(held, offset, -1), axis=1, keepdims=True)
        first = jnp.where(low > 90, -1, low)
        second = jnp.where(high > low, high, -1)
        table = jnp.where(lane == 2 * l, first, jnp.where(lane == 2 * l + 1, second, table))
    turned = jnp.transpose(table)[:8]
    return jnp.concatenate([turned, jnp.full((8, 96), -1, jnp.int32)], axis=1)


def kernel(
    q_hbm, k_hbm, v_hbm, mk_hbm, mv_hbm, ids_hbm, gw_hbm, gb_hbm,
    out_hbm,
    out_ref, q_buf, kv_buf, mem_buf, tab_buf, tab_sm,
    part_buf, lse_buf, in_buf, in_lse, z_part, z_lse, z_in, z_lse_in,
    loc_fin, mem_fin, acc_ref, max_ref, lg_out, lg_in, ids_ref, gw_ref, gb_ref,
    l_sem, kvz_s, kvz_r, kva_s, kva_r, qb_s, qb_r, qz_s, qz_r, tab_s, tab_r, ma_s, ma_r,
    rs_s, rs_r, rl_s, rl_r, z_s, z_r, zs_s, zs_r, lg_s, lg_r,
):
    c = lax.axis_index("ctx")
    g_own = lax.axis_index("mem")
    x, y, z = c // 8, (c // 2) % 4, c % 2
    zo = 1 - z

    def wrap(i):
        return lax.rem(i + SIDE, SIDE)

    def device(px, py, pz):
        return (px * 8 + py * 2 + pz, g_own)

    def key_peer(h, d):
        return device(wrap(x + d), y, z) if h == 0 else device(x, wrap(y + d), z)

    def query_peer(h, d):
        if isinstance(h, int):
            return key_peer(1 - h, d)
        px = jnp.where(h == 0, x, wrap(x + d))
        return device(px, jnp.where(h == 0, wrap(y + d), y), z)

    def query_own(h):
        return b_own[h] if isinstance(h, int) else jnp.where(h == 0, y, x)

    z_peer = device(x, y, zo)
    a_own = (x, y)
    b_own = (y, x)

    def remote(src, dst, ssem, rsem, peer):
        return pltpu.make_async_remote_copy(
            src_ref=src, dst_ref=dst, send_sem=ssem, recv_sem=rsem,
            device_id=peer, device_id_type=MESH,
        )

    kv_local, q_local, mem_local, small_local = [], [], [], []
    count = 0

    def local(src, dst, group):
        nonlocal count
        cp = pltpu.make_async_copy(src, dst, l_sem.at[count])
        cp.start()
        group.append(cp)
        count += 1

    for h in range(2):
        cols = pl.ds(h * DH, DH)
        local(k_hbm.at[:, cols], kv_buf.at[h, a_own[h], 0, z], kv_local)
        local(v_hbm.at[:, cols], kv_buf.at[h, a_own[h], 1, z], kv_local)
    for h in range(2):
        for g in range(SHARE):
            local(
                q_hbm.at[:, pl.ds((h * SHARE + g) * DH, DH)],
                q_buf.at[h, b_own[h], z, g],
                q_local,
            )
    for h in range(2):
        cols = pl.ds(h * DH, DH)
        local(mk_hbm.at[:, :, cols], mem_buf.at[h, a_own[h], 0], mem_local)
        local(mv_hbm.at[:, :, cols], mem_buf.at[h, a_own[h], 1], mem_local)

    local(ids_hbm, ids_ref, small_local)
    local(gw_hbm, gw_ref, small_local)
    local(gb_hbm, gb_ref, small_local)

    barrier = pltpu.get_barrier_semaphore()
    greeted = [z_peer]
    for d in (1, 3):
        greeted += [device(wrap(x + d), y, z), device(x, wrap(y + d), z)]
    for d in range(1, GROUPS):
        greeted += [(c, lax.rem(g_own + d, GROUPS))]
    for peer in greeted:
        pl.semaphore_signal(barrier, inc=1, device_id=peer, device_id_type=MESH)
    pl.semaphore_wait(barrier, len(greeted))

    started = []

    def go(cp):
        cp.start()
        started.append(cp)
        return cp

    def kv_z(h):
        ref = kv_buf.at[h, a_own[h], :, z]
        return remote(ref, ref, kvz_s.at[h], kvz_r.at[h], z_peer)

    def kv_z_in(h):
        ref = kv_buf.at[h, a_own[h], :, zo]
        return remote(ref, ref, kvz_s.at[h], kvz_r.at[h], z_peer)

    def ring(h, own, peer, ref, ssem, rsem):
        left, right, across = wrap(own - 1), wrap(own + 1), wrap(own + 2)
        out = [(own, 0, 1), (own, 1, 3), (own, 1, 1), (own, 0, 3), (left, 0, 1), (right, 1, 3)]
        come = [(left, 0), (right, 1), (left, 1), (right, 0), (across, 0), (across, 1)]

        def copy(n):
            at, half, d = out[n]
            return remote(ref(at, half), ref(at, half), ssem.at[n], rsem.at[n], peer(h, d))

        def send(n):
            copy(n).start()

        def sent(n):
            copy(n).wait_send()

        def wait(n):
            at, half = come[n]
            remote(ref(at, half), ref(at, half), ssem.at[n], rsem.at[n], z_peer).wait_recv()

        return send, wait, sent

    def kv_ring(h, part):
        pz = (z, zo)[part]
        return ring(
            h, a_own[h], key_peer, lambda at, half: kv_buf.at[h, at, half, pz],
            kva_s.at[h, part], kva_r.at[h, part],
        )

    def q_ring(h):
        return ring(
            h, b_own[h], query_peer, lambda at, half: q_buf.at[h, at, z, pl.ds(2 * half, 2)],
            qb_s.at[h], qb_r.at[h],
        )

    def mem_ring(h, part):
        blocks = pl.ds(part * (SHARD_BLOCKS // 2), SHARD_BLOCKS // 2)
        return ring(
            h, a_own[h], key_peer, lambda at, half: mem_buf.at[h, at, half, blocks],
            ma_s.at[h, part], ma_r.at[h, part],
        )

    def q_z(h, d):
        ref = q_buf.at[h, wrap(b_own[h] + d), z]
        return remote(ref, ref, qz_s.at[h, d], qz_r.at[h, d], z_peer)

    def q_z_in(h, d):
        ref = q_buf.at[h, wrap(b_own[h] + d), zo]
        return remote(ref, ref, qz_s.at[h, d], qz_r.at[h, d], z_peer)

    def tab(h, n, at, pz, peer):
        ref = tab_buf.at[h, wrap(b_own[h] + at), pz]
        return remote(ref, ref, tab_s.at[h, n], tab_r.at[h, n], peer)

    def tab_out(h, n):
        at, way = ((0, 1), (0, 3), (-1, 1))[n]
        return tab(h, n, at, z, query_peer(h, way))

    def tab_in(h, n):
        return tab(h, n, (-1, 1, 2)[n], z, z_peer)

    def tab_z(h, d, pz):
        return tab(h, 3 + d, d, pz, z_peer)

    q_rings = [q_ring(h) for h in range(2)]
    kv_rings = [kv_ring(h, 0) for h in range(2)]
    kvo_rings = [kv_ring(h, 1) for h in range(2)]
    mem_a_rings = [mem_ring(h, 0) for h in range(2)]
    mem_b_rings = [mem_ring(h, 1) for h in range(2)]

    def on(rings, what, *steps):
        for n in steps:
            for r in rings:
                r[what](n)

    SEND, WAIT, SENT = 0, 1, 2
    for cp in kv_local:
        cp.wait()
    for h in range(2):
        go(kv_z(h))
    for cp in q_local:
        cp.wait()
    on(q_rings, SEND, 0, 1)
    on(kv_rings, SEND, 0, 1)
    on(q_rings, SEND, 2, 3)
    on(kv_rings, SEND, 2, 3)
    for h in range(2):
        go(q_z(h, 0))
    for cp in mem_local:
        cp.wait()
    on(mem_a_rings, SEND, 0, 1)
    for cp in small_local:
        cp.wait()
    for h in range(2):
        tab_buf[h, b_own[h], z] = block_table(ids_ref[...])
    for h in range(2):
        go(tab_out(h, 0))
        go(tab_out(h, 1))
        go(tab_z(h, 0, z))
    for h in range(2):
        kv_z_in(h).wait_recv()
    on(kvo_rings, SEND, 0, 1, 2, 3)
    on(q_rings, WAIT, 0, 1)
    on(q_rings, SEND, 4, 5)
    on(kv_rings, WAIT, 0, 1)
    on(kv_rings, SEND, 4, 5)
    on(mem_a_rings, SEND, 2, 3)
    on(q_rings, WAIT, 2, 3)
    for h in range(2):
        go(q_z(h, 1))
        go(q_z(h, 3))
    on(kvo_rings, WAIT, 0, 1)
    on(kvo_rings, SEND, 4, 5)
    for h in range(2):
        tab_in(h, 0).wait_recv()
        tab_in(h, 1).wait_recv()
        go(tab_out(h, 2))
        go(tab_z(h, 3, z))
        go(tab_z(h, 1, z))
    on(mem_b_rings, SEND, 0, 1, 2, 3)
    on(q_rings, WAIT, 4, 5)
    for h in range(2):
        go(q_z(h, 2))
    on(kv_rings, WAIT, 2, 3, 4, 5)
    on(kvo_rings, WAIT, 2, 3, 4, 5)
    for h in range(2):
        tab_in(h, 2).wait_recv()
        go(tab_z(h, 2, z))
    for n in range(2):
        for r in mem_a_rings:
            r[WAIT](n)
            r[SEND](4 + n)

    def local_shard(h, d):
        b = wrap(b_own[h] + d)
        if h == 0:
            tiles = x + jnp.where(y <= b, 1, 0)
            q_shard = (x * 4 + b) * 2 + z
        else:
            tiles = jnp.where(x < b, 4, jnp.where(x == b, y + 1, 0))
            q_shard = (b * 4 + y) * 2 + z
        lane_blk = lax.broadcasted_iota(jnp.int32, (1, 512), 1) // QBLK

        acc_ref[...] = jnp.zeros_like(acc_ref)
        max_ref[...] = jnp.full_like(max_ref, NEG)

        def tile(a, carry):
            k_shard = (a * 4 + y) * 2 if h == 0 else (x * 4 + a) * 2
            keys = kv_buf[h, a, 0].reshape(512, DH)
            vals = with_ones(kv_buf[h, a, 1].reshape(512, DH))
            for blk in range(2):
                seen = k_shard * 2 + lane_blk <= q_shard * 2 + blk
                bias = jnp.where(seen, 0.0, NEG)
                for g in range(SHARE):
                    n = blk * SHARE + g
                    q = q_buf[h, b, z, g, blk * QBLK : (blk + 1) * QBLK, :]
                    s = dot_nt(q, keys) + bias
                    old = max_ref[n]
                    new = jnp.maximum(old, jnp.max(s, axis=1, keepdims=True))
                    wide = jnp.concatenate([new] * 4, axis=1)
                    p = jnp.exp2((s - wide) * FACTOR).astype(jnp.bfloat16)
                    fade = jnp.exp2((old - new) * FACTOR)
                    add = jnp.dot(p, vals, preferred_element_type=jnp.float32)
                    acc_ref[n, :, :DH] = acc_ref[n, :, :DH] * fade + add[:, :DH]
                    acc_ref[n, :, DH:] = acc_ref[n, :, DH:] * fade + add[:, DH:]
                    max_ref[n] = new
            return carry

        lax.fori_loop(0, tiles, tile, 0)
        for blk in range(2):
            tok = slice(blk * QBLK, (blk + 1) * QBLK)
            sums = []
            for g in range(SHARE):
                n = blk * SHARE + g
                total = acc_ref[n, :, DH:]
                some = total > 0.0
                safe = jnp.where(some, total, 1.0)
                part_buf[0, h, b, g, tok, :] = (acc_ref[n, :, :DH] / safe).astype(jnp.bfloat16)
                sums.append(jnp.where(some, max_ref[n] * FACTOR + jnp.log2(safe), NEG))
            lse_buf[0, h, b, 0, :, tok] = rows_of(sums[:2])
            lse_buf[0, h, b, 1, :, tok] = rows_of(sums[2:])

    MESSAGES = [(2, 0, 1, 0), (2, 1, 3, 0), (1, 1, 1, 1), (3, 0, 3, 2), (1, 0, 1, 1), (3, 1, 3, 2)]

    def result_copies(job, h, n, whose, half, way, lands):
        b = wrap(query_own(h) + whose)
        heads = pl.ds(2 * half, 2)
        peer = query_peer(h, way)
        return (
            remote(
                part_buf.at[job, h, b, heads], in_buf.at[job, h, lands, heads],
                rs_s.at[job, h, n], rs_r.at[job, h, n], peer,
            ),
            remote(
                lse_buf.at[job, h, b, half], in_lse.at[job, h, lands, half],
                rl_s.at[job, h, n], rl_r.at[job, h, n], peer,
            ),
        )

    def send_results(job, *numbers):
        for n in numbers:
            for h in range(2):
                for cp in result_copies(job, h, n, *MESSAGES[n]):
                    cp.start()

    def each_pair(body, init=0):
        for m in range(4):
            init = body(m % 2, m // 2, init)
        return init

    def weights(stats):
        top = functools.reduce(jnp.maximum, stats)
        powers = [jnp.exp2(s - top) for s in stats]
        total = functools.reduce(jnp.add, powers)
        scales = [jnp.transpose(p / total) for p in powers]
        return scales, top + jnp.log2(total)

    def merge(parts, scales, half, k):
        total = None
        for part, scale in zip(parts, scales):
            term = part[2 * half + k].astype(jnp.float32) * scale[:, k : k + 1]
            total = term if total is None else total + term
        return total

    def pass_on(job):
        def pair(h, half, carry):
            way = 1 + 2 * half
            for cp in result_copies(job, h, half, 2, half, way, 0):
                cp.wait_recv()
            b = wrap(query_own(h) + way)
            mine, other = part_buf.at[job, h, b], in_buf.at[job, h, 0]
            scales, whole = weights([lse_buf[job, h, b, half], in_lse[job, h, 0, half]])
            for k in range(2):
                mine[2 * half + k] = merge([mine, other], scales, half, k).astype(jnp.bfloat16)
            lse_buf[job, h, b, half] = whole
            for cp in result_copies(job, h, 4 + half, way, half, way, 1 + half):
                cp.start()
            return carry

        each_pair(pair)

    def finish(job, h, half, more_parts=(), more_stats=()):
        b = query_own(h)
        left, right = jnp.where(half == 0, 4, 2), jnp.where(half == 0, 3, 5)
        for n, lands in ((left, 1), (right, 2)):
            for cp in result_copies(job, h, n, 0, half, 1, lands):
                cp.wait_recv()
        parts = [part_buf.at[job, h, b], in_buf.at[job, h, 1], in_buf.at[job, h, 2], *more_parts]
        stats = [lse_buf[job, h, b, half], in_lse[job, h, 1, half], in_lse[job, h, 2, half], *more_stats]
        scales, whole = weights(stats)
        return [merge(parts, scales, half, k) for k in range(2)], whole

    def order(i):
        return jnp.where(i == 0, 2, jnp.where(i == 1, 1, jnp.where(i == 2, 3, 0)))

    def local_step(i, carry):
        for h in range(2):
            local_shard(h, order(i))
        @pl.when(i == 0)
        def _():
            send_results(0, 0, 1)
            for n in range(2):
                for r in mem_b_rings:
                    r[WAIT](n)
                    r[SEND](4 + n)

        pl.when(i == 1)(lambda: send_results(0, 2))
        pl.when(i == 2)(lambda: send_results(0, 3))
        return carry

    lax.fori_loop(0, SIDE, local_step, 0)

    for h in range(2):
        for d in range(SIDE):
            tab_z(h, d, zo).wait_recv()
    to_smem = pltpu.make_async_copy(tab_buf, tab_sm, l_sem.at[count])
    to_smem.start()
    to_smem.wait()
    on(mem_a_rings, WAIT, 2, 3, 4, 5)
    on(mem_b_rings, WAIT, 2, 3, 4, 5)
    for h in range(2):
        for d in range(SIDE):
            q_z_in(h, d).wait_recv()

    lane = lax.broadcasted_iota(jnp.int32, (1, 2 * MBLK), 1)

    def memory_shard(job, h, b, pz):
        for blk in range(2):
            tok = slice(blk * QBLK, (blk + 1) * QBLK)
            keys, vals, bias = [], [], []
            for a in range(SIDE):
                shard = (a * 4 + y) * 2 + z if h == 0 else (x * 4 + a) * 2 + z
                slots = [tab_sm[h, b, pz, 2 * blk + k, shard] for k in range(2)]
                for slot in slots:
                    at = jnp.clip(slot, 0, SHARD_BLOCKS - 1)
                    keys.append(mem_buf[h, a, 0, at])
                    vals.append(mem_buf[h, a, 1, at])
                off = [jnp.where(slot < 0, NEG, 0.0) for slot in slots]
                bias.append(jnp.where(lane < MBLK, off[0], off[1]))
            keys = jnp.concatenate(keys, axis=0)
            vals = with_ones(jnp.concatenate(vals, axis=0))
            bias = jnp.concatenate(bias, axis=1)
            sums = []
            for g in range(SHARE):
                s = dot_nt(q_buf[h, b, pz, g, tok, :], keys) + bias
                top = jnp.max(s, axis=1, keepdims=True)
                p = jnp.exp2((s - top) * FACTOR).astype(jnp.bfloat16)
                both = jnp.dot(p, vals, preferred_element_type=jnp.float32)
                total = both[:, DH:]
                part_buf[job, h, b, g, tok, :] = (both[:, :DH] / total).astype(jnp.bfloat16)
                sums.append(top * FACTOR + jnp.log2(total))
            lse_buf[job, h, b, 0, :, tok] = rows_of(sums[:2])
            lse_buf[job, h, b, 1, :, tok] = rows_of(sums[2:])

    def z_copies(h, half):
        heads = pl.ds(2 * half, 2)
        n = 2 * h + half
        return (
            remote(z_part.at[h, heads], z_in.at[h, heads], z_s.at[n], z_r.at[n], z_peer),
            remote(z_lse.at[h, half], z_lse_in.at[h, half], zs_s.at[n], zs_r.at[n], z_peer),
        )

    def to_z_peer():
        def pair(h, half, carry):
            results, whole = finish(1, h, half)
            for k in range(2):
                z_part[h, 2 * half + k] = results[k].astype(jnp.bfloat16)
            z_lse[h, half] = whole
            for cp in z_copies(h, half):
                cp.start()
            return carry

        each_pair(pair)

    def memory_step(i, carry):
        job = 1 + i // SIDE
        for h in range(2):
            memory_shard(job, h, wrap(b_own[h] + order(i % SIDE)), jnp.where(job == 1, zo, z))
        pl.when(i == 0)(lambda: send_results(1, 0, 1))
        pl.when(i == 1)(lambda: send_results(1, 2))
        pl.when(i == 2)(lambda: send_results(1, 3))
        pl.when(i == 3)(lambda: pass_on(1))
        pl.when(i == 4)(lambda: send_results(2, 0, 1))
        pl.when(i == 5)(lambda: send_results(2, 2))
        pl.when(i == 5)(to_z_peer)
        pl.when(i == 6)(lambda: send_results(2, 3))
        pl.when(i == 6)(lambda: pass_on(0))
        pl.when(i == 7)(lambda: pass_on(2))
        return carry

    lax.fori_loop(0, 2 * SIDE, memory_step, 0)

    def gate_dot(which, fin, head):
        feats = pl.ds(pl.multiple_of(head * DH, DH), DH)
        return dot_nt(gw_ref[which, :, feats], fin[head].astype(jnp.bfloat16))

    def local_pair(h, half, logits):
        results, _ = finish(0, h, half)
        for k in range(2):
            head = h * SHARE + 2 * half + k
            loc_fin[head] = results[k]
            logits += gate_dot(0, loc_fin, head)
        return logits

    def memory_pair(h, half, logits):
        for cp in z_copies(h, half):
            cp.wait_recv()
        results, _ = finish(2, h, half, [z_in.at[h]], [z_lse_in[h, half]])
        for k in range(2):
            head = h * SHARE + 2 * half + k
            mem_fin[head] = results[k]
            logits += gate_dot(1, mem_fin, head)
        return logits

    logits = each_pair(local_pair, jnp.zeros((GROUPS * HEADS_DEV, ROWS), jnp.float32))
    logits = each_pair(memory_pair, logits)
    lg_out[...] = logits.reshape(GROUPS, HEADS_DEV, ROWS)

    def lg(d):
        to = lax.rem(g_own + d, GROUPS)
        return remote(lg_out.at[to], lg_in.at[d], lg_s.at[d], lg_r.at[d], (c, to))

    for d in range(1, GROUPS):
        go(lg(d))
    own = lg_out[g_own]
    for d in range(1, GROUPS):
        lg(d).wait_recv()
        own = own + lg_in[d]
    go_out = []
    gate = jax.nn.sigmoid(jnp.transpose(own) + gb_ref[...])
    for head in range(HEADS_DEV):
        share = gate[:, head : head + 1]
        mixed = share * mem_fin[head] + (1.0 - share) * loc_fin[head]
        out_ref[:, head * DH : (head + 1) * DH] = mixed.astype(jnp.bfloat16)
        if head % 4 == 3:
            cols = pl.ds((head - 3) * DH, 4 * DH)
            done = pltpu.make_async_copy(out_ref.at[:, cols], out_hbm.at[:, cols], l_sem.at[head // 4])
            go_out.append(done)
            done.start()

    for h in range(2):
        for job in range(3):
            for n in range(6):
                for cp in result_copies(job, h, n, *MESSAGES[n]):
                    cp.wait_send()
        for half in range(2):
            for cp in z_copies(h, half):
                cp.wait_send()
    for rings in (q_rings, kv_rings, kvo_rings, mem_a_rings, mem_b_rings):
        on(rings, SENT, *range(6))
    for cp in started:
        cp.wait_send()
    for cp in go_out:
        cp.wait()


def on_device(queries, keys, values, mem_keys, mem_values, retrieval, gate_weight, gate_bias):
    bf, f32 = jnp.bfloat16, jnp.float32
    dma = pltpu.SemaphoreType.DMA
    hbm = pl.BlockSpec(memory_space=pltpu.HBM)
    vmem = pl.BlockSpec(memory_space=pltpu.VMEM)
    part = (SHARE, ROWS, DH)
    stat = (8, ROWS)
    return pl.pallas_call(
        kernel,
        out_shape=jax.ShapeDtypeStruct((ROWS, HEADS_DEV * DH), bf),
        in_specs=[hbm] * 8,
        out_specs=hbm,
        scratch_shapes=[
            pltpu.VMEM((ROWS, HEADS_DEV * DH), bf),
            pltpu.VMEM((2, SIDE, 2) + part, bf),
            pltpu.VMEM((2, SIDE, 2, 2, ROWS, DH), bf),
            pltpu.VMEM((2, SIDE, 2, SHARD_BLOCKS, MBLK, DH), bf),
            pltpu.VMEM((2, SIDE, 2, 8, 128), jnp.int32),
            pltpu.SMEM((2, SIDE, 2, 8, 128), jnp.int32),
            pltpu.VMEM((3, 2, SIDE) + part, bf),
            pltpu.VMEM((3, 2, SIDE, 2) + stat, f32),
            pltpu.VMEM((3, 2, 3) + part, bf),
            pltpu.VMEM((3, 2, 3, 2) + stat, f32),
            pltpu.VMEM((2,) + part, bf),
            pltpu.VMEM((2, 2) + stat, f32),
            pltpu.VMEM((2,) + part, bf),
            pltpu.VMEM((2, 2) + stat, f32),
            pltpu.VMEM((HEADS_DEV, ROWS, DH), f32),
            pltpu.VMEM((HEADS_DEV, ROWS, DH), f32),
            pltpu.VMEM((2 * SHARE, QBLK, 2 * DH), f32),
            pltpu.VMEM((2 * SHARE, QBLK, DH), f32),
            pltpu.VMEM((GROUPS, HEADS_DEV, ROWS), f32),
            pltpu.VMEM((GROUPS, HEADS_DEV, ROWS), f32),
            pltpu.VMEM((2, 32), jnp.int32),
            pltpu.VMEM((2, GROUPS * HEADS_DEV, HEADS_DEV * DH), bf),
            pltpu.VMEM((1, HEADS_DEV), f32),
            dma((24,)),
            dma((2,)), dma((2,)),
            dma((2, 2, 6)), dma((2, 2, 6)),
            dma((2, 6)), dma((2, 6)),
            dma((2, SIDE)), dma((2, SIDE)),
            dma((2, 8)), dma((2, 8)),
            dma((2, 2, 6)), dma((2, 2, 6)),
            dma((3, 2, 6)), dma((3, 2, 6)),
            dma((3, 2, 6)), dma((3, 2, 6)),
            dma((4,)), dma((4,)),
            dma((4,)), dma((4,)),
            dma((SIDE,)), dma((SIDE,)),
        ],
        compiler_params=pltpu.CompilerParams(
            collective_id=0, has_side_effects=True, vmem_limit_bytes=60 * 2**20
        ),
    )(
        queries, keys, values, mem_keys, mem_values, retrieval.reshape(2, -1),
        gate_weight.transpose(0, 2, 1), gate_bias.reshape(1, HEADS_DEV),
    )


def solution(mesh):
    placed = (
        P("ctx", "mem"),
        P("ctx", "mem"),
        P("ctx", "mem"),
        P("ctx", None, "mem"),
        P("ctx", None, "mem"),
        P("ctx", "mem", None),
        P(None, "mem", None),
        P("mem"),
    )
    return jax.shard_map(
        on_device, mesh=mesh, in_specs=placed, out_specs=P("ctx", "mem"), check_vma=False
    )
```
